32 devices in a mesh: groups: 2 (over y), row: 4 (over z), col: 2 (over x), depth: 2 (over core).
Axes of the slice: x: 2, y: 2, z: 4, core: 2. Of those that a mesh axis runs over, the one named last changes fastest.
Arguments:
- density: float32 [512, 4096], P(('groups', 'row', 'col', 'depth')), parts along dimension 0, may hold values from -0.8 to 0.8
- square_left: int32 [32768], P(('groups', 'row', 'col', 'depth')), parts along dimension 0, may hold values from 0 to 63
- square_right: int32 [32768], P(('groups', 'row', 'col', 'depth')), parts along dimension 0, may hold values from 0 to 63
- square_out: int32 [32768], P(('groups', 'row', 'col', 'depth')), parts along dimension 0, may hold values from 0 to 31
- square_count: int32 [32], P(('groups', 'row', 'col', 'depth')), parts along dimension 0, may hold values from 128 to 1024, as said below
- cube_left: int32 [32768], P(('groups', 'row', 'col', 'depth')), parts along dimension 0, may hold values from 0 to 63
- cube_right: int32 [32768], P(('groups', 'row', 'col', 'depth')), parts along dimension 0, may hold values from 0 to 63
- cube_out: int32 [32768], P(('groups', 'row', 'col', 'depth')), parts along dimension 0, may hold values from 0 to 31
- cube_count: int32 [32], P(('groups', 'row', 'col', 'depth')), parts along dimension 0, may hold values from 128 to 1024, as said below
Outputs:
- purified: float32 [512, 4096], P(('groups', 'row', 'col', 'depth')), parts along dimension 0
The draws below stay inside these ranges and needn't reach their ends.
There are 2 independent parts, one for each index of `groups`. The reference program is written for one: setup_inputs(seed, part) draws one part's arguments, and reference() takes and returns one part's arrays. A program takes and returns all parts, laid end to end along the dimension named above; each array names one. Nothing has to cross between parts.
Inputs may be any that keep to these rules, and one draw needn't show every extreme that they name: `square_count`: each device has an eighth, a quarter, a half or all of 1024 live tasks, and some device of every copy has all 1024. `cube_count`: as for square_count.
All inputs are finite; a program needn't handle non-finite values.
Results may differ from the reference program's by a relative error of at most 0.0003.
Values sent between devices are 32-bit elements; how exact they have to be, the bound alone decides.
No kernel may reach another device: no remote copies, remote signals or barrier semaphores. Data moves between devices by JAX's collectives and lax.ppermute only.
A program may use at most 64 MiB of HBM per device.

```python
import jax
import jax.numpy as jnp
from jax import lax

BLOCK = 64
BLK_DEV = 16
OUT_DEV = 16
TASKS = 1024
BLOCK_AREA = 4096
SLOTS = 256
TASK_ALL = 16384
N_ROW = 4
N_COL = 2
N_DEPTH = 2


def live_counts(key):
    devs = N_ROW * N_COL * N_DEPTH
    first, second = jax.random.split(key)
    power = jax.random.randint(first, (devs,), 0, 4)
    counts = jnp.right_shift(jnp.full((devs,), TASKS, jnp.int32), power.astype(jnp.int32))
    top = jax.random.randint(second, (), 0, devs)
    return jnp.where(jnp.arange(devs, dtype=jnp.int32) == top, TASKS, counts).astype(jnp.int32)


def draw_square_count(key, part):
    key = jax.random.fold_in(key, 11)
    return live_counts(key)


def draw_cube_count(key, part):
    key = jax.random.fold_in(key, 23)
    return live_counts(key)


def with_ends(result, stream_key, least, top_value):
    extent = result.shape
    spot = [jax.random.randint(jax.random.fold_in(stream_key, axis), (), 0, extent[axis]) for axis in range(len(extent))]
    result = result.at[tuple(spot)].set(least)
    longest = extent.index(max(extent))
    spot[longest] = (spot[longest] + 1) % extent[longest]
    return result.at[tuple(spot)].set(top_value)


def shard_levels(rng, dims, cuts, least, top_value):
    level = 1.0
    for dim, shards_of in cuts:
        heights = jax.random.uniform(jax.random.fold_in(jax.random.fold_in(rng, 6), dim), (shards_of,), jnp.float32, least / len(cuts), top_value / len(cuts))
        level = level * jnp.repeat(jnp.exp(heights), dims[dim] // shards_of).reshape((-1,) + (1,) * (len(dims) - 1 - dim))
    return level


def normal_values(own_key, shape, deviation, most, pieces=(), held_as=jnp.bfloat16):
    level = shard_levels(own_key, shape, pieces, -0.22, 0.18) if pieces else 1.0
    drawn = jax.random.normal(own_key, shape, jnp.float32) * deviation * level
    return jnp.minimum(jnp.maximum(drawn, -most), most).astype(held_as)


def setup_inputs(seed: int = 0, part: int = 0) -> dict:
    arg_keys = jax.random.split(jax.random.key(seed), 10)
    own_keys = jax.random.split(jax.random.fold_in(arg_keys[9], part), 10)
    density = normal_values(own_keys[0], (SLOTS, BLOCK_AREA), 0.1, 0.8, ((0, 16),), jnp.float32)
    square_left = with_ends(jax.random.randint(own_keys[1], (TASK_ALL,), 0, N_COL * N_DEPTH * BLK_DEV), jax.random.fold_in(own_keys[1], 1), 0, (N_COL * N_DEPTH * BLK_DEV) - 1).astype(jnp.int32)
    square_right = with_ends(jax.random.randint(own_keys[2], (TASK_ALL,), 0, N_ROW * BLK_DEV), jax.random.fold_in(own_keys[2], 1), 0, (N_ROW * BLK_DEV) - 1).astype(jnp.int32)
    square_out = with_ends(jax.random.randint(own_keys[3], (TASK_ALL,), 0, N_DEPTH * OUT_DEV), jax.random.fold_in(own_keys[3], 1), 0, (N_DEPTH * OUT_DEV) - 1).astype(jnp.int32)
    square_count = draw_square_count(jax.random.fold_in(jax.random.fold_in(arg_keys[9], part), 71), part)
    cube_left = with_ends(jax.random.randint(own_keys[5], (TASK_ALL,), 0, N_COL * N_DEPTH * OUT_DEV), jax.random.fold_in(own_keys[5], 1), 0, (N_COL * N_DEPTH * OUT_DEV) - 1).astype(jnp.int32)
    cube_right = with_ends(jax.random.randint(own_keys[6], (TASK_ALL,), 0, N_ROW * BLK_DEV), jax.random.fold_in(own_keys[6], 1), 0, (N_ROW * BLK_DEV) - 1).astype(jnp.int32)
    cube_out = with_ends(jax.random.randint(own_keys[7], (TASK_ALL,), 0, N_DEPTH * OUT_DEV), jax.random.fold_in(own_keys[7], 1), 0, (N_DEPTH * OUT_DEV) - 1).astype(jnp.int32)
    cube_count = draw_cube_count(jax.random.fold_in(jax.random.fold_in(arg_keys[9], part), 71), part)
    return dict(density=density, square_left=square_left, square_right=square_right, square_out=square_out, square_count=square_count, cube_left=cube_left, cube_right=cube_right, cube_out=cube_out, cube_count=cube_count)


def tile_sum(left, right, left_index, right_index, out_index, count, slots):
    side = BLOCK
    live = (jnp.arange(TASKS, dtype=jnp.int32) < count).astype(jnp.float32)
    first = left[left_index].reshape(TASKS, side, side)
    second = right[right_index].reshape(TASKS, side, side)
    product = jnp.einsum("tij,tjk->tik", first, second, precision=lax.Precision.HIGHEST).reshape(TASKS, side * side)
    onehot = (out_index[:, None] == jnp.arange(slots, dtype=jnp.int32)[None, :]).astype(jnp.float32) * live[:, None]
    return jnp.dot(onehot.T, product, precision=lax.Precision.HIGHEST)


def layered(blocks, per_dev, task_left, task_right, task_out, counts, right_grid):
    grid = blocks.reshape(N_ROW, N_COL, N_DEPTH, per_dev, BLOCK * BLOCK)
    slots = N_DEPTH * OUT_DEV

    def one_device(items):
        index, lefts, rights, outs, count = items
        row_id = index // (N_COL * N_DEPTH)
        col_id = (index // N_DEPTH) % N_COL
        layer = index % N_DEPTH
        left = lax.dynamic_index_in_dim(grid, row_id, 0, keepdims=False).reshape(-1, BLOCK * BLOCK)
        right = lax.dynamic_index_in_dim(right_grid, col_id, 1, keepdims=False)
        right = lax.dynamic_index_in_dim(right, layer, 1, keepdims=False).reshape(-1, BLOCK * BLOCK)
        return tile_sum(left, right, lefts, rights, outs, count, slots)

    shape = (N_ROW * N_COL * N_DEPTH, TASKS)
    partial_value = lax.map(one_device, (jnp.arange(N_ROW * N_COL * N_DEPTH, dtype=jnp.int32), task_left.reshape(shape), task_right.reshape(shape), task_out.reshape(shape), counts))
    partial_value = partial_value.reshape(N_ROW, N_COL, N_DEPTH, N_DEPTH, OUT_DEV, BLOCK * BLOCK)
    return jnp.sum(partial_value, axis=2).reshape(N_ROW * N_COL * N_DEPTH * OUT_DEV, BLOCK * BLOCK)


def reference(density, square_left, square_right, square_out, square_count, cube_left, cube_right, cube_out, cube_count):
    right_grid = density.reshape(N_ROW, N_COL, N_DEPTH, BLK_DEV, BLOCK * BLOCK)
    square = layered(density, BLK_DEV, square_left, square_right, square_out, square_count, right_grid)
    cube = layered(square, OUT_DEV, cube_left, cube_right, cube_out, cube_count, right_grid)
    return 3.0 * square - 2.0 * cube
```

```python
import functools
import math

import jax
import jax.numpy as jnp
from jax import lax
from jax.experimental import pallas as pl
from jax.experimental.pallas import tpu as pltpu
from jax.sharding import PartitionSpec as P

OUT_DEV = 16
CHUNK = 8
TURN = 4


def ring(value, axis):
    size = lax.axis_size(axis)
    return lax.ppermute(value, axis, [(i, (i + 1) % size) for i in range(size)])


def ring_all(value, axis):
    pieces = [value]
    for _ in range(lax.axis_size(axis) - 1):
        pieces.append(ring(pieces[-1], axis))
    return pieces


def plan(key, left, out, groups, seg_groups, slots, chunks):
    tasks = key.shape[0]
    place = jnp.arange(tasks, dtype=jnp.int32)
    group = jnp.arange(groups, dtype=jnp.int32)
    segs = groups // seg_groups
    same = (key[:, None] == key[None, :]) & (place[:, None] < place[None, :])
    rank = jnp.sum(same.astype(jnp.int32), axis=0)
    count = jnp.sum((key[:, None] == group[None, :]).astype(jnp.int32), axis=0)
    filled = (count + CHUNK - 1) // CHUNK
    seg_id = group // seg_groups
    earlier = (group[:, None] < group[None, :]) & (seg_id[:, None] == seg_id[None, :])
    within = jnp.sum(jnp.where(earlier, filled[:, None], 0), axis=0)
    total = jnp.sum(filled.reshape(segs, seg_groups), axis=1)
    turns = (total + TURN - 1) // TURN
    seg = jnp.arange(segs, dtype=jnp.int32)
    first = jnp.sum(jnp.where(seg[:, None] < seg[None, :], turns[:, None], 0), axis=0)
    base = within + TURN * jnp.sum(
        jnp.where(seg_id[:, None] == seg[None, :], first[None, :], 0), axis=1
    )
    start = jnp.sum(jnp.where(key[:, None] == group[None, :], base[None, :] * CHUNK, 0), axis=1)
    position = jnp.where(key < groups, start + rank, -1)
    slot = jnp.arange(chunks * CHUNK, dtype=jnp.int32)
    code = jnp.sum(
        jnp.where(
            position[:, None] == slot[None, :], (left * (slots + 1) + out - slots)[:, None], 0
        ),
        axis=0,
    ) + slots
    chunk = jnp.arange(chunks, dtype=jnp.int32)
    rights = jnp.sum((base + filled)[:, None] <= chunk[None, :], axis=0, dtype=jnp.int32)
    return dict(
        first=first,
        turns=turns,
        rights=rights,
        left=code // (slots + 1) * 32,
        out=code % (slots + 1) * 32,
    )


def kernel(raw_lefts, raw_rights, has_left, has_right, has_sum, last, slots, first_group, refs):
    refs = list(refs)
    meta, rights, lefts, outs = refs[:4]
    refs = refs[4:]
    left_raw, refs = refs[:raw_lefts], refs[raw_lefts:]
    right_raw, refs = refs[:raw_rights], refs[raw_rights:]
    panel, given, sum_in = None, [], None
    if has_left:
        panel, refs = refs[0], refs[1:]
    given, refs = refs[:has_right], refs[has_right:]
    if has_sum:
        sum_in, refs = refs[0], refs[1:]
    results, refs = refs[:2] if last else refs[:1], refs[2:] if last else refs[1:]
    if raw_lefts:
        panel, refs = refs[0], refs[1:]
    if raw_rights:
        weights, refs = refs[0], refs[1:]
    else:
        weights = given[0]
    flat, tall, sum_0, sum_1 = refs
    sums = (sum_0, sum_1)
    low = lax.broadcasted_iota(jnp.int32, (32, 128), 1) < 64

    def spread(source):
        for high in range(0, source.shape[0], 8):
            for pair in range(32):
                flat[pl.ds(high * 32 + pair, 8, stride=32), :] = source[
                    high : high + 8, pair * 128 : pair * 128 + 128
                ]

    def split(value):
        top = value.astype(jnp.bfloat16)
        return top, (value - top.astype(jnp.float32)).astype(jnp.bfloat16)

    for index, source in enumerate(left_raw):
        spread(source)
        for block in range(16):
            top, rest = split(flat[block * 32 : block * 32 + 32, :])
            panel[pl.ds(index * 512 + block * 32, 32), 0:128] = top
            panel[pl.ds(index * 512 + block * 32, 32), 128:256] = rest
    for index, source in enumerate(right_raw):
        spread(source)
        for block in range(16):
            both = flat[block * 32 : block * 32 + 32, :]
            swapped = pltpu.roll(both, 64, 1)
            spot = block % 4 * 128
            tall[pl.ds(spot, 32, stride=2), :] = jnp.where(low, both, 0.0)
            tall[pl.ds(spot + 1, 32, stride=2), :] = jnp.where(low, swapped, 0.0)
            tall[pl.ds(spot + 64, 32, stride=2), :] = jnp.where(low, 0.0, swapped)
            tall[pl.ds(spot + 65, 32, stride=2), :] = jnp.where(low, 0.0, both)
            top, rest = split(tall[spot : spot + 128, :])
            weights[index * 16 + block, 0] = top
            weights[index * 16 + block, 1] = rest

    sum_1[...] = jnp.zeros_like(sum_1)
    if has_sum:
        sum_0[...] = sum_in[...]
    else:
        sum_0[...] = jnp.zeros_like(sum_0)

    zero = jnp.zeros((128, 128), jnp.bfloat16)
    limit = weights.shape[0] - 1
    most = panel.shape[0] - 32

    def issue(chunk, unit, total):
        right = jnp.clip(rights[chunk] - first_group, 0, limit)
        top, rest = weights[right, 0], weights[right, 1]
        pltpu.matmul_push_rhs(
            jnp.concatenate(
                [jnp.concatenate([top, rest], 1), jnp.concatenate([top, zero], 1)], 0
            ),
            0,
            unit,
        )
        rows = [
            panel[pl.ds(pl.multiple_of(jnp.minimum(lefts[chunk * CHUNK + task], most), 32), 32), :]
            for task in range(CHUNK)
        ]
        pltpu.matmul_acc_lhs(total, jnp.concatenate(rows, 0), load_staged_rhs=0)

    def drain(chunk, unit, total):
        product = pltpu.matmul_pop(total)
        product = product[:, :128] + product[:, 128:]
        for task in range(CHUNK):
            rows = pl.ds(pl.multiple_of(outs[chunk * CHUNK + task], 32), 32)
            sums[unit][rows, :] += product[task * 32 : task * 32 + 32]

    def work(*totals):
        begin, turns = meta[0] * TURN, meta[1]
        for unit in range(2):
            issue(begin + unit, unit, totals[unit])

        @pl.loop(0, turns)
        def _(turn):
            chunk = begin + turn * TURN
            for unit in range(2):
                issue(chunk + 2 + unit, unit, totals[2 + unit])
            for unit in range(2):
                drain(chunk + unit, unit, totals[unit])
            for unit in range(2):
                issue(chunk + 4 + unit, unit, totals[unit])
            for unit in range(2):
                drain(chunk + 2 + unit, unit, totals[2 + unit])

        for unit in range(2):
            pltpu.matmul_pop(totals[unit])

    pl.run_scoped(
        work,
        *[pltpu.ACC(unit)((CHUNK * 32, 256), jnp.float32) for _ in range(2) for unit in range(2)],
    )

    if not last:
        results[0][...] = sum_0[...] + sum_1[...]
        return
    sum_0[...] = sum_0[...] + sum_1[...]
    layer = meta[2]
    size = results[0].shape[0]
    layers = slots // size
    for index, result in enumerate(results):
        row = (layer * size if index == 0 else lax.rem(layer + 1, layers) * size) * 32
        for high in range(0, size, 8):
            for pair in range(32):
                result[high : high + 8, pair * 128 : pair * 128 + 128] = sum_0[
                    pl.ds(row + high * 32 + pair, 8, stride=32), :
                ]


def tile_sum(tasks, seg, seg_count, left_raw, right_raw, panel, given, sum_in, last, slots, width, first_group):
    f32, bf16 = jnp.float32, jnp.bfloat16
    turns = tasks["turns"][seg]
    for other in range(seg + 1, seg + seg_count):
        turns = turns + tasks["turns"][other]
    meta = jnp.stack([tasks["first"][seg], turns, lax.axis_index("depth")]).astype(jnp.int32)
    args = [meta, tasks["rights"], tasks["left"], tasks["out"], *left_raw, *right_raw]
    smem, vmem = pl.BlockSpec(memory_space=pltpu.SMEM), pl.BlockSpec(memory_space=pltpu.VMEM)
    extra = [v for v in [panel, *given, sum_in] if v is not None]
    in_specs = [smem] * 4 + [vmem] * (len(left_raw) + len(right_raw) + len(extra))
    sum_shape = ((slots + 1) * 32, 128)
    shapes = (
        [jax.ShapeDtypeStruct((OUT_DEV, width), f32)] * 2
        if last
        else [jax.ShapeDtypeStruct(sum_shape, f32)]
    )
    if left_raw:
        shapes.append(jax.ShapeDtypeStruct((len(left_raw) * 512, 256), bf16))
    if right_raw:
        shapes.append(jax.ShapeDtypeStruct((len(right_raw) * 16, 2, 128, 128), bf16))
    body = functools.partial(
        kernel,
        len(left_raw),
        len(right_raw),
        panel is not None,
        len(given),
        sum_in is not None,
        last,
        slots,
        first_group,
    )
    return pl.pallas_call(
        lambda *refs: body(refs),
        out_shape=shapes,
        in_specs=in_specs,
        out_specs=[vmem] * len(shapes),
        scratch_shapes=[
            pltpu.VMEM((512, 128), f32),
            pltpu.VMEM((512, 128), f32),
            pltpu.VMEM(sum_shape, f32),
            pltpu.VMEM(sum_shape, f32),
        ],
        compiler_params=pltpu.CompilerParams(vmem_limit_bytes=44 << 20),
    )(*args, *extra)


def local(
    density,
    square_left,
    square_right,
    square_out,
    square_count,
    cube_left,
    cube_right,
    cube_out,
    cube_count,
):
    per_dev, width = density.shape
    rows, cols, layers = (lax.axis_size(name) for name in ("row", "col", "depth"))
    row, col, layer = (lax.axis_index(name) for name in ("row", "col", "depth"))
    slots = layers * OUT_DEV
    tasks = square_left.shape[0]
    place = jnp.arange(tasks, dtype=jnp.int32)

    def moved_left(left):
        from_col = lax.rem(col - left // (layers * per_dev) + cols, cols)
        from_layer = lax.rem(layer - left // per_dev % layers + layers, layers)
        return from_col, (from_col * layers + from_layer) * per_dev + left % per_dev

    def moved_right(right):
        return lax.rem(row - right // per_dev + rows, rows) * per_dev + right % per_dev

    column = ring_all(density, "row")
    across = ring_all(density, "col")
    lefts = [piece for value in across for piece in ring_all(value, "depth")]

    groups = rows * per_dev
    _, left = moved_left(square_left)
    key = jnp.where(place < square_count[0], moved_right(square_right), groups)
    chunks = -(-(tasks // CHUNK + groups + TURN * rows + TURN) // 16) * 16
    square_tasks = plan(key, left, square_out, groups, per_dev, slots, chunks)
    from_col, left = moved_left(cube_left)
    left = left - jnp.where(from_col == 0, 0, layers * per_dev)
    key = jnp.where(from_col == 0, 0, groups) + moved_right(cube_right)
    key = jnp.where(place < cube_count[0], key, 2 * groups)
    chunks = -(-(tasks // CHUNK + 2 * groups + TURN * 2 + TURN) // 16) * 16
    cube_tasks = plan(key, left, cube_out, 2 * groups, groups, slots, chunks)

    total, panel, first = tile_sum(
        square_tasks, 0, 2, lefts, column[:2], None, [], None, False, slots, width, 0
    )
    weights = [first]
    for seg in range(2, rows):
        *result, piece = tile_sum(
            square_tasks, seg, 1, [], [column[seg]], panel, [], total, seg == rows - 1,
            slots, width, seg * per_dev,
        )
        total = result[0]
        weights.append(piece)
    mine, other = result
    weights = jnp.concatenate(weights, axis=0)
    square = mine + ring(other, "depth")

    squares = [piece for value in ring_all(square, "col") for piece in ring_all(value, "depth")]
    total, near = tile_sum(
        cube_tasks, 0, 1, squares[:layers], [], None, [weights], None, False, slots, width, 0
    )
    mine, other, _ = tile_sum(
        cube_tasks, 1, 1, squares[layers:], [], None, [weights], total, True, slots, width, groups
    )
    cube = mine + ring(other, "depth")
    return 3.0 * square - 2.0 * cube


def solution(mesh):
    return jax.shard_map(
        local,
        mesh=mesh,
        in_specs=(
            P(("groups", "row", "col", "depth"), None),
            P(("groups", "row", "col", "depth")),
            P(("groups", "row", "col", "depth")),
            P(("groups", "row", "col", "depth")),
            P(("groups", "row", "col", "depth")),
            P(("groups", "row", "col", "depth")),
            P(("groups", "row", "col", "depth")),
            P(("groups", "row", "col", "depth")),
            P(("groups", "row", "col", "depth")),
        ),
        out_specs=P(("groups", "row", "col", "depth"), None),
        check_vma=False,
    )
```

```python
import functools
import math

import jax
import jax.numpy as jnp
from jax import lax
from jax.experimental import pallas as pl
from jax.experimental.pallas import tpu as pltpu
from jax.sharding import PartitionSpec as P

OUT_DEV = 16
CHUNK = 8
TURN = 4


def ring(value, axis):
    size = lax.axis_size(axis)
    return lax.ppermute(value, axis, [(i, (i + 1) % size) for i in range(size)])


def ring_all(value, axis):
    pieces = [value]
    for _ in range(lax.axis_size(axis) - 1):
        pieces.append(ring(pieces[-1], axis))
    return pieces


def plan(key, left, out, groups, seg_groups, slots, chunks):
    tasks = key.shape[0]
    place = jnp.arange(tasks, dtype=jnp.int32)
    group = jnp.arange(groups, dtype=jnp.int32)
    segs = groups // seg_groups
    same = (key[:, None] == key[None, :]) & (place[:, None] < place[None, :])
    rank = jnp.sum(same.astype(jnp.int32), axis=0)
    count = jnp.sum((key[:, None] == group[None, :]).astype(jnp.int32), axis=0)
    filled = (count + CHUNK - 1) // CHUNK
    seg_id = group // seg_groups
    earlier = (group[:, None] < group[None, :]) & (seg_id[:, None] == seg_id[None, :])
    within = jnp.sum(jnp.where(earlier, filled[:, None], 0), axis=0)
    total = jnp.sum(filled.reshape(segs, seg_groups), axis=1)
    turns = (total + TURN - 1) // TURN
    seg = jnp.arange(segs, dtype=jnp.int32)
    first = jnp.sum(jnp.where(seg[:, None] < seg[None, :], turns[:, None], 0), axis=0)
    base = within + TURN * jnp.sum(
        jnp.where(seg_id[:, None] == seg[None, :], first[None, :], 0), axis=1
    )
    start = jnp.sum(jnp.where(key[:, None] == group[None, :], base[None, :] * CHUNK, 0), axis=1)
    position = jnp.where(key < groups, start + rank, -1)
    slot = jnp.arange(chunks * CHUNK, dtype=jnp.int32)
    code = jnp.sum(
        jnp.where(
            position[:, None] == slot[None, :], (left * (slots + 1) + out - slots)[:, None], 0
        ),
        axis=0,
    ) + slots
    chunk = jnp.arange(chunks, dtype=jnp.int32)
    rights = jnp.sum((base + filled)[:, None] <= chunk[None, :], axis=0, dtype=jnp.int32)
    return dict(
        first=first,
        turns=turns,
        rights=rights,
        left=code // (slots + 1) * 32,
        out=code % (slots + 1) * 32,
    )


def kernel(raw_lefts, raw_rights, has_left, has_right, has_sum, last, slots, first_group, segs, refs):
    refs = list(refs)
    first, turn_count, rights, lefts, outs = refs[:5]
    refs = refs[5:]
    left_raw, refs = refs[:raw_lefts], refs[raw_lefts:]
    right_raw, refs = refs[:raw_rights], refs[raw_rights:]
    panel, given, sum_in = None, [], None
    if has_left:
        panel, refs = refs[0], refs[1:]
    given, refs = refs[:has_right], refs[has_right:]
    if has_sum:
        sum_in, refs = refs[0], refs[1:]
    results, refs = refs[:2] if last else refs[:1], refs[2:] if last else refs[1:]
    if raw_lefts:
        panel, refs = refs[0], refs[1:]
    if raw_rights:
        weights, refs = refs[0], refs[1:]
    else:
        weights = given[0]
    flat, tall, sum_0, sum_1 = refs
    sums = (sum_0, sum_1)
    low = lax.broadcasted_iota(jnp.int32, (32, 128), 1) < 64

    def spread(source):
        for high in range(0, source.shape[0], 8):
            for pair in range(32):
                flat[pl.ds(high * 32 + pair, 8, stride=32), :] = source[
                    high : high + 8, pair * 128 : pair * 128 + 128
                ]

    def split(value):
        top = value.astype(jnp.bfloat16)
        return top, (value - top.astype(jnp.float32)).astype(jnp.bfloat16)

    for index, source in enumerate(left_raw):
        spread(source)
        for block in range(16):
            top, rest = split(flat[block * 32 : block * 32 + 32, :])
            panel[pl.ds(index * 512 + block * 32, 32), 0:128] = top
            panel[pl.ds(index * 512 + block * 32, 32), 128:256] = rest
    for index, source in enumerate(right_raw):
        spread(source)
        for block in range(16):
            both = flat[block * 32 : block * 32 + 32, :]
            swapped = pltpu.roll(both, 64, 1)
            spot = block % 4 * 128
            tall[pl.ds(spot, 32, stride=2), :] = jnp.where(low, both, 0.0)
            tall[pl.ds(spot + 1, 32, stride=2), :] = jnp.where(low, swapped, 0.0)
            tall[pl.ds(spot + 64, 32, stride=2), :] = jnp.where(low, 0.0, swapped)
            tall[pl.ds(spot + 65, 32, stride=2), :] = jnp.where(low, 0.0, both)
            top, rest = split(tall[spot : spot + 128, :])
            weights[index * 16 + block, 0] = top
            weights[index * 16 + block, 1] = rest

    sum_1[...] = jnp.zeros_like(sum_1)
    if has_sum:
        sum_0[...] = sum_in[...]
    else:
        sum_0[...] = jnp.zeros_like(sum_0)

    zero = jnp.zeros((128, 128), jnp.bfloat16)
    limit = weights.shape[0] - 1
    most = panel.shape[0] - 32

    def issue(chunk, unit, total):
        right = jnp.clip(rights[chunk] - first_group, 0, limit)
        top, rest = weights[right, 0], weights[right, 1]
        pltpu.matmul_push_rhs(
            jnp.concatenate(
                [jnp.concatenate([top, rest], 1), jnp.concatenate([top, zero], 1)], 0
            ),
            0,
            unit,
        )
        rows = [
            panel[pl.ds(pl.multiple_of(jnp.minimum(lefts[chunk * CHUNK + task], most), 32), 32), :]
            for task in range(CHUNK)
        ]
        pltpu.matmul_acc_lhs(total, jnp.concatenate(rows, 0), load_staged_rhs=0)

    def drain(chunk, unit, total):
        product = pltpu.matmul_pop(total)
        product = product[:, :128] + product[:, 128:]
        for task in range(CHUNK):
            rows = pl.ds(pl.multiple_of(outs[chunk * CHUNK + task], 32), 32)
            sums[unit][rows, :] += product[task * 32 : task * 32 + 32]

    def work(*totals):
        begin, turns = first[segs[0]] * TURN, turn_count[segs[0]]
        for seg in segs[1:]:
            turns = turns + turn_count[seg]
        for unit in range(2):
            issue(begin + unit, unit, totals[unit])

        @pl.loop(0, turns)
        def _(turn):
            chunk = begin + turn * TURN
            for unit in range(2):
                issue(chunk + 2 + unit, unit, totals[2 + unit])
            for unit in range(2):
                drain(chunk + unit, unit, totals[unit])
            for unit in range(2):
                issue(chunk + 4 + unit, unit, totals[unit])
            for unit in range(2):
                drain(chunk + 2 + unit, unit, totals[2 + unit])

        for unit in range(2):
            pltpu.matmul_pop(totals[unit])

    pl.run_scoped(
        work,
        *[pltpu.ACC(unit)((CHUNK * 32, 256), jnp.float32) for _ in range(2) for unit in range(2)],
    )

    if not last:
        results[0][...] = sum_0[...] + sum_1[...]
        return
    sum_0[...] = sum_0[...] + sum_1[...]
    layer = lax.axis_index("depth")
    size = results[0].shape[0]
    layers = slots // size
    for index, result in enumerate(results):
        row = (layer * size if index == 0 else lax.rem(layer + 1, layers) * size) * 32
        for high in range(0, size, 8):
            for pair in range(32):
                result[high : high + 8, pair * 128 : pair * 128 + 128] = sum_0[
                    pl.ds(row + high * 32 + pair, 8, stride=32), :
                ]


def tile_sum(tasks, seg, seg_count, left_raw, right_raw, panel, given, sum_in, last, slots, width, first_group):
    f32, bf16 = jnp.float32, jnp.bfloat16
    plans = [tasks[name] for name in ("first", "turns", "rights", "left", "out")]
    args = [*plans, *left_raw, *right_raw]
    smem, vmem = pl.BlockSpec(memory_space=pltpu.SMEM), pl.BlockSpec(memory_space=pltpu.VMEM)
    extra = [v for v in [panel, *given, sum_in] if v is not None]
    in_specs = [smem] * 5 + [vmem] * (len(left_raw) + len(right_raw) + len(extra))
    sum_shape = ((slots + 1) * 32, 128)
    shapes = (
        [jax.ShapeDtypeStruct((OUT_DEV, width), f32)] * 2
        if last
        else [jax.ShapeDtypeStruct(sum_shape, f32)]
    )
    if left_raw:
        shapes.append(jax.ShapeDtypeStruct((len(left_raw) * 512, 256), bf16))
    if right_raw:
        shapes.append(jax.ShapeDtypeStruct((len(right_raw) * 16, 2, 128, 128), bf16))
    body = functools.partial(
        kernel,
        len(left_raw),
        len(right_raw),
        panel is not None,
        len(given),
        sum_in is not None,
        last,
        slots,
        first_group,
        tuple(range(seg, seg + seg_count)),
    )
    return pl.pallas_call(
        lambda *refs: body(refs),
        out_shape=shapes,
        in_specs=in_specs,
        out_specs=[vmem] * len(shapes),
        scratch_shapes=[
            pltpu.VMEM((512, 128), f32),
            pltpu.VMEM((512, 128), f32),
            pltpu.VMEM(sum_shape, f32),
            pltpu.VMEM(sum_shape, f32),
        ],
        compiler_params=pltpu.CompilerParams(vmem_limit_bytes=44 << 20),
    )(*args, *extra)


def local(
    density,
    square_left,
    square_right,
    square_out,
    square_count,
    cube_left,
    cube_right,
    cube_out,
    cube_count,
):
    per_dev, width = density.shape
    rows, cols, layers = (lax.axis_size(name) for name in ("row", "col", "depth"))
    row, col, layer = (lax.axis_index(name) for name in ("row", "col", "depth"))
    slots = layers * OUT_DEV
    tasks = square_left.shape[0]
    place = jnp.arange(tasks, dtype=jnp.int32)

    def moved_left(left):
        from_col = lax.rem(col - left // (layers * per_dev) + cols, cols)
        from_layer = lax.rem(layer - left // per_dev % layers + layers, layers)
        return from_col, (from_col * layers + from_layer) * per_dev + left % per_dev

    def moved_right(right):
        return lax.rem(row - right // per_dev + rows, rows) * per_dev + right % per_dev

    column = ring_all(density, "row")
    across = ring_all(density, "col")
    lefts = [piece for value in across for piece in ring_all(value, "depth")]

    groups = rows * per_dev
    _, left = moved_left(square_left)
    key = jnp.where(place < square_count[0], moved_right(square_right), groups)
    chunks = -(-(tasks // CHUNK + groups + TURN * rows + TURN) // 16) * 16
    square_tasks = plan(key, left, square_out, groups, per_dev, slots, chunks)
    cube_left, cube_right, cube_out, cube_count, _ = lax.optimization_barrier(
        (cube_left, cube_right, cube_out, cube_count, column[1])
    )
    from_col, left = moved_left(cube_left)
    left = left - jnp.where(from_col == 0, 0, layers * per_dev)
    key = jnp.where(from_col == 0, 0, groups) + moved_right(cube_right)
    key = jnp.where(place < cube_count[0], key, 2 * groups)
    chunks = -(-(tasks // CHUNK + 2 * groups + TURN * 2 + TURN) // 16) * 16
    cube_tasks = plan(key, left, cube_out, 2 * groups, groups, slots, chunks)

    total, panel, first = tile_sum(
        square_tasks, 0, 2, lefts, column[:2], None, [], None, False, slots, width, 0
    )
    weights = [first]
    for seg in range(2, rows):
        *result, piece = tile_sum(
            square_tasks, seg, 1, [], [column[seg]], panel, [], total, seg == rows - 1,
            slots, width, seg * per_dev,
        )
        total = result[0]
        weights.append(piece)
    mine, other = result
    weights = jnp.concatenate(weights, axis=0)
    square = mine + ring(other, "depth")

    near = ring_all(square, "depth")
    far = ring_all(square, "col")[1:]
    total, _ = tile_sum(
        cube_tasks, 0, 1, near, [], None, [weights], None, False, slots, width, 0
    )
    total, *far = lax.optimization_barrier((total, *far))
    far = [piece for value in far for piece in ring_all(value, "depth")]
    mine, other, _ = tile_sum(
        cube_tasks, 1, 1, far, [], None, [weights], total, True, slots, width, groups
    )
    cube = mine + ring(other, "depth")
    return 3.0 * square - 2.0 * cube


def solution(mesh):
    return jax.shard_map(
        local,
        mesh=mesh,
        in_specs=(
            P(("groups", "row", "col", "depth"), None),
            P(("groups", "row", "col", "depth")),
            P(("groups", "row", "col", "depth")),
            P(("groups", "row", "col", "depth")),
            P(("groups", "row", "col", "depth")),
            P(("groups", "row", "col", "depth")),
            P(("groups", "row", "col", "depth")),
            P(("groups", "row", "col", "depth")),
            P(("groups", "row", "col", "depth")),
        ),
        out_specs=P(("groups", "row", "col", "depth"), None),
        check_vma=False,
    )
```

```python
import functools
import math

import jax
import jax.numpy as jnp
from jax import lax
from jax.experimental import pallas as pl
from jax.experimental.pallas import tpu as pltpu
from jax.sharding import PartitionSpec as P

OUT_DEV = 16
CHUNK = 8
TURN = 4


def ring(value, axis, step=1):
    size = lax.axis_size(axis)
    return lax.ppermute(value, axis, [(i, (i + step) % size) for i in range(size)])


def ring_all(value, axis):
    pieces = [value]
    for _ in range(lax.axis_size(axis) - 1):
        pieces.append(ring(pieces[-1], axis))
    return pieces


def plan(key, left, out, groups, seg_groups, slots, chunks):
    tasks = key.shape[0]
    place = jnp.arange(tasks, dtype=jnp.int32)
    group = jnp.arange(groups, dtype=jnp.int32)
    segs = groups // seg_groups
    same = (key[:, None] == key[None, :]) & (place[:, None] < place[None, :])
    rank = jnp.sum(same.astype(jnp.int32), axis=0)
    count = jnp.sum((key[:, None] == group[None, :]).astype(jnp.int32), axis=0)
    filled = (count + CHUNK - 1) // CHUNK
    seg_id = group // seg_groups
    earlier = (group[:, None] < group[None, :]) & (seg_id[:, None] == seg_id[None, :])
    within = jnp.sum(jnp.where(earlier, filled[:, None], 0), axis=0)
    total = jnp.sum(filled.reshape(segs, seg_groups), axis=1)
    turns = (total + TURN - 1) // TURN
    seg = jnp.arange(segs, dtype=jnp.int32)
    first = jnp.sum(jnp.where(seg[:, None] < seg[None, :], turns[:, None], 0), axis=0)
    base = within + TURN * jnp.sum(
        jnp.where(seg_id[:, None] == seg[None, :], first[None, :], 0), axis=1
    )
    start = jnp.sum(jnp.where(key[:, None] == group[None, :], base[None, :] * CHUNK, 0), axis=1)
    position = jnp.where(key < groups, start + rank, -1)
    slot = jnp.arange(chunks * CHUNK, dtype=jnp.int32)
    code = jnp.sum(
        jnp.where(
            position[:, None] == slot[None, :], (left * (slots + 1) + out - slots)[:, None], 0
        ),
        axis=0,
    ) + slots
    chunk = jnp.arange(chunks, dtype=jnp.int32)
    rights = jnp.sum((base + filled)[:, None] <= chunk[None, :], axis=0, dtype=jnp.int32)
    return dict(
        first=first,
        turns=turns,
        rights=rights,
        left=code // (slots + 1) * 32,
        out=code % (slots + 1) * 32,
    )


def kernel(raw_lefts, raw_rights, has_left, has_right, has_sum, last, slots, first_group, segs, halves, refs):
    refs = list(refs)
    first, turn_count, rights, lefts, outs = refs[:5]
    refs = refs[5:]
    left_raw, refs = refs[:raw_lefts], refs[raw_lefts:]
    spots = raw_rights * 2 if halves else raw_rights
    right_raw, refs = refs[:spots], refs[spots:]
    panel, given, sum_in = None, [], None
    if has_left:
        panel, refs = refs[0], refs[1:]
    given, refs = refs[:has_right], refs[has_right:]
    if has_sum:
        sum_in, refs = refs[0], refs[1:]
    results, refs = refs[:2] if last else refs[:1], refs[2:] if last else refs[1:]
    if raw_lefts:
        panel, refs = refs[0], refs[1:]
    if raw_rights:
        weights, refs = refs[0], refs[1:]
    else:
        weights = given[0]
    flat, tall, sum_0, sum_1 = refs
    sums = (sum_0, sum_1)
    low = lax.broadcasted_iota(jnp.int32, (32, 128), 1) < 64

    def spread(source, block=0):
        for high in range(0, source.shape[0], 8):
            for pair in range(32):
                flat[pl.ds((block + high) * 32 + pair, 8, stride=32), :] = source[
                    high : high + 8, pair * 128 : pair * 128 + 128
                ]

    def split(value):
        top = value.astype(jnp.bfloat16)
        return top, (value - top.astype(jnp.float32)).astype(jnp.bfloat16)

    for index, source in enumerate(left_raw):
        spread(source)
        for block in range(16):
            top, rest = split(flat[block * 32 : block * 32 + 32, :])
            panel[pl.ds(index * 512 + block * 32, 32), 0:128] = top
            panel[pl.ds(index * 512 + block * 32, 32), 128:256] = rest
    for index in range(raw_rights):
        parts = right_raw[index * 2 : index * 2 + 2] if halves else right_raw[index : index + 1]
        for part, source in enumerate(parts):
            spread(source, part * 8)
        for block in range(16):
            both = flat[block * 32 : block * 32 + 32, :]
            swapped = pltpu.roll(both, 64, 1)
            spot = block % 4 * 128
            tall[pl.ds(spot, 32, stride=2), :] = jnp.where(low, both, 0.0)
            tall[pl.ds(spot + 1, 32, stride=2), :] = jnp.where(low, swapped, 0.0)
            tall[pl.ds(spot + 64, 32, stride=2), :] = jnp.where(low, 0.0, swapped)
            tall[pl.ds(spot + 65, 32, stride=2), :] = jnp.where(low, 0.0, both)
            top, rest = split(tall[spot : spot + 128, :])
            weights[index * 16 + block, 0] = top
            weights[index * 16 + block, 1] = rest

    sum_1[...] = jnp.zeros_like(sum_1)
    if has_sum:
        sum_0[...] = sum_in[...]
    else:
        sum_0[...] = jnp.zeros_like(sum_0)

    zero = jnp.zeros((128, 128), jnp.bfloat16)
    limit = weights.shape[0] - 1
    most = panel.shape[0] - 32

    def issue(chunk, unit, total):
        right = jnp.clip(rights[chunk] - first_group, 0, limit)
        top, rest = weights[right, 0], weights[right, 1]
        pltpu.matmul_push_rhs(
            jnp.concatenate(
                [jnp.concatenate([top, rest], 1), jnp.concatenate([top, zero], 1)], 0
            ),
            0,
            unit,
        )
        rows = [
            panel[pl.ds(pl.multiple_of(jnp.minimum(lefts[chunk * CHUNK + task], most), 32), 32), :]
            for task in range(CHUNK)
        ]
        pltpu.matmul_acc_lhs(total, jnp.concatenate(rows, 0), load_staged_rhs=0)

    def drain(chunk, unit, total):
        product = pltpu.matmul_pop(total)
        product = product[:, :128] + product[:, 128:]
        for task in range(CHUNK):
            rows = pl.ds(pl.multiple_of(outs[chunk * CHUNK + task], 32), 32)
            sums[unit][rows, :] += product[task * 32 : task * 32 + 32]

    def work(*totals):
        begin, turns = first[segs[0]] * TURN, turn_count[segs[0]]
        for seg in segs[1:]:
            turns = turns + turn_count[seg]
        for unit in range(2):
            issue(begin + unit, unit, totals[unit])

        @pl.loop(0, turns)
        def _(turn):
            chunk = begin + turn * TURN
            for unit in range(2):
                issue(chunk + 2 + unit, unit, totals[2 + unit])
            for unit in range(2):
                drain(chunk + unit, unit, totals[unit])
            for unit in range(2):
                issue(chunk + 4 + unit, unit, totals[unit])
            for unit in range(2):
                drain(chunk + 2 + unit, unit, totals[2 + unit])

        for unit in range(2):
            pltpu.matmul_pop(totals[unit])

    pl.run_scoped(
        work,
        *[pltpu.ACC(unit)((CHUNK * 32, 256), jnp.float32) for _ in range(2) for unit in range(2)],
    )

    if not last:
        results[0][...] = sum_0[...] + sum_1[...]
        return
    sum_0[...] = sum_0[...] + sum_1[...]
    layer = lax.axis_index("depth")
    size = results[0].shape[0]
    layers = slots // size
    for index, result in enumerate(results):
        row = (layer * size if index == 0 else lax.rem(layer + 1, layers) * size) * 32
        for high in range(0, size, 8):
            for pair in range(32):
                result[high : high + 8, pair * 128 : pair * 128 + 128] = sum_0[
                    pl.ds(row + high * 32 + pair, 8, stride=32), :
                ]


def tile_sum(tasks, seg, seg_count, left_raw, right_raw, panel, given, sum_in, last, slots, width, first_group, halves=False):
    f32, bf16 = jnp.float32, jnp.bfloat16
    rights = len(right_raw) // 2 if halves else len(right_raw)
    plans = [tasks[name] for name in ("first", "turns", "rights", "left", "out")]
    args = [*plans, *left_raw, *right_raw]
    smem, vmem = pl.BlockSpec(memory_space=pltpu.SMEM), pl.BlockSpec(memory_space=pltpu.VMEM)
    extra = [v for v in [panel, *given, sum_in] if v is not None]
    in_specs = [smem] * 5 + [vmem] * (len(left_raw) + len(right_raw) + len(extra))
    sum_shape = ((slots + 1) * 32, 128)
    shapes = (
        [jax.ShapeDtypeStruct((OUT_DEV, width), f32)] * 2
        if last
        else [jax.ShapeDtypeStruct(sum_shape, f32)]
    )
    if left_raw:
        shapes.append(jax.ShapeDtypeStruct((len(left_raw) * 512, 256), bf16))
    if right_raw:
        shapes.append(jax.ShapeDtypeStruct((rights * 16, 2, 128, 128), bf16))
    body = functools.partial(
        kernel,
        len(left_raw),
        rights,
        panel is not None,
        len(given),
        sum_in is not None,
        last,
        slots,
        first_group,
        tuple(range(seg, seg + seg_count)),
        halves,
    )
    return pl.pallas_call(
        lambda *refs: body(refs),
        out_shape=shapes,
        in_specs=in_specs,
        out_specs=[vmem] * len(shapes),
        scratch_shapes=[
            pltpu.VMEM((512, 128), f32),
            pltpu.VMEM((512, 128), f32),
            pltpu.VMEM(sum_shape, f32),
            pltpu.VMEM(sum_shape, f32),
        ],
        compiler_params=pltpu.CompilerParams(vmem_limit_bytes=44 << 20),
    )(*args, *extra)


def local(
    density,
    square_left,
    square_right,
    square_out,
    square_count,
    cube_left,
    cube_right,
    cube_out,
    cube_count,
):
    per_dev, width = density.shape
    rows, cols, layers = (lax.axis_size(name) for name in ("row", "col", "depth"))
    row, col, layer = (lax.axis_index(name) for name in ("row", "col", "depth"))
    slots = layers * OUT_DEV
    tasks = square_left.shape[0]
    place = jnp.arange(tasks, dtype=jnp.int32)

    def moved_left(left):
        from_col = lax.rem(col - left // (layers * per_dev) + cols, cols)
        from_layer = lax.rem(layer - left // per_dev % layers + layers, layers)
        return from_col, (from_col * layers + from_layer) * per_dev + left % per_dev

    def moved_right(right):
        away = lax.rem(row - right // per_dev + rows, rows)
        order = jnp.where(
            2 * away <= rows - 1 + rows % 2, 2 * away - 1, jnp.minimum(2 * (rows - away), rows - 1)
        )
        return jnp.maximum(order, 0) * per_dev + right % per_dev

    column = [density]
    for _ in range((rows - 1) // 2):
        ahead, behind = (column[-2], column[-1]) if len(column) > 1 else (density, density)
        column += [ring(ahead, "row"), ring(behind, "row", -1)]
    across = ring_all(density, "col")
    lefts = [piece for value in across for piece in ring_all(value, "depth")]

    groups = rows * per_dev
    _, left = moved_left(square_left)
    key = jnp.where(place < square_count[0], moved_right(square_right), groups)
    chunks = -(-(tasks // CHUNK + groups + TURN * rows + TURN) // 16) * 16
    square_tasks = plan(key, left, square_out, groups, per_dev, slots, chunks)
    from_col, left = moved_left(cube_left)
    left = left - jnp.where(from_col == 0, 0, layers * per_dev)
    key = jnp.where(from_col == 0, 0, groups) + moved_right(cube_right)
    key = jnp.where(place < cube_count[0], key, 2 * groups)
    chunks = -(-(tasks // CHUNK + 2 * groups + TURN * 2 + TURN) // 16) * 16
    cube_tasks = plan(key, left, cube_out, 2 * groups, groups, slots, chunks)

    total, panel, first = tile_sum(
        square_tasks, 0, 1, lefts, column[:1], None, [], None, False, slots, width, 0
    )
    weights = [first]
    half = per_dev // 2
    if rows % 2 == 0:
        ahead, behind, total = lax.optimization_barrier((*column[-2:], total))
        column[-2:] = [ahead, behind]
        opposite = [ring(ahead[:half], "row"), ring(behind[half:], "row", -1)]
    for seg in range(1, len(column), 2):
        last = rows % 2 == 1 and seg + 2 == rows
        *result, piece = tile_sum(
            square_tasks, seg, 2, [], column[seg : seg + 2], panel, [], total, last,
            slots, width, seg * per_dev,
        )
        total = result[0]
        weights.append(piece)
    if rows % 2 == 0:
        *result, piece = tile_sum(
            square_tasks, rows - 1, 1, [], opposite, panel, [], total, True,
            slots, width, (rows - 1) * per_dev, True,
        )
        weights.append(piece)
    mine, other = result
    weights = jnp.concatenate(weights, axis=0)
    square = mine + ring(other, "depth")

    near = ring_all(square, "depth")
    far = ring_all(square, "col")[1:]
    total, _ = tile_sum(
        cube_tasks, 0, 1, near, [], None, [weights], None, False, slots, width, 0
    )
    total, *far = lax.optimization_barrier((total, *far))
    far = [piece for value in far for piece in ring_all(value, "depth")]
    mine, other, _ = tile_sum(
        cube_tasks, 1, 1, far, [], None, [weights], total, True, slots, width, groups
    )
    cube = mine + ring(other, "depth")
    return 3.0 * square - 2.0 * cube


def solution(mesh):
    return jax.shard_map(
        local,
        mesh=mesh,
        in_specs=(
            P(("groups", "row", "col", "depth"), None),
            P(("groups", "row", "col", "depth")),
            P(("groups", "row", "col", "depth")),
            P(("groups", "row", "col", "depth")),
            P(("groups", "row", "col", "depth")),
            P(("groups", "row", "col", "depth")),
            P(("groups", "row", "col", "depth")),
            P(("groups", "row", "col", "depth")),
            P(("groups", "row", "col", "depth")),
        ),
        out_specs=P(("groups", "row", "col", "depth"), None),
        check_vma=False,
    )
```

```python
import functools
import math

import jax
import jax.numpy as jnp
from jax import lax
from jax.experimental import pallas as pl
from jax.experimental.pallas import tpu as pltpu
from jax.sharding import PartitionSpec as P

OUT_DEV = 16
CHUNK = 8
TURN = 4


def ring(value, axis, step=1):
    size = lax.axis_size(axis)
    return lax.ppermute(value, axis, [(i, (i + step) % size) for i in range(size)])


def ring_all(value, axis):
    pieces = [value]
    for _ in range(lax.axis_size(axis) - 1):
        pieces.append(ring(pieces[-1], axis))
    return pieces


def plan(key, left, out, groups, seg_groups, slots, chunks):
    tasks = key.shape[0]
    place = jnp.arange(tasks, dtype=jnp.int32)
    group = jnp.arange(groups, dtype=jnp.int32)
    segs = groups // seg_groups
    same = (key[:, None] == key[None, :]) & (place[:, None] < place[None, :])
    rank = jnp.sum(same.astype(jnp.int32), axis=0)
    count = jnp.sum((key[:, None] == group[None, :]).astype(jnp.int32), axis=0)
    filled = (count + CHUNK - 1) // CHUNK
    seg_id = group // seg_groups
    earlier = (group[:, None] < group[None, :]) & (seg_id[:, None] == seg_id[None, :])
    within = jnp.sum(jnp.where(earlier, filled[:, None], 0), axis=0)
    total = jnp.sum(filled.reshape(segs, seg_groups), axis=1)
    turns = (total + TURN - 1) // TURN
    seg = jnp.arange(segs, dtype=jnp.int32)
    first = jnp.sum(jnp.where(seg[:, None] < seg[None, :], turns[:, None], 0), axis=0)
    base = within + TURN * jnp.sum(
        jnp.where(seg_id[:, None] == seg[None, :], first[None, :], 0), axis=1
    )
    start = jnp.sum(jnp.where(key[:, None] == group[None, :], base[None, :] * CHUNK, 0), axis=1)
    position = jnp.where(key < groups, start + rank, -1)
    slot = jnp.arange(chunks * CHUNK, dtype=jnp.int32)
    code = jnp.sum(
        jnp.where(
            position[:, None] == slot[None, :], (left * (slots + 1) + out - slots)[:, None], 0
        ),
        axis=0,
    ) + slots
    chunk = jnp.arange(chunks, dtype=jnp.int32)
    rights = jnp.sum((base + filled)[:, None] <= chunk[None, :], axis=0, dtype=jnp.int32)
    return dict(
        first=first,
        turns=turns,
        rights=rights,
        left=code // (slots + 1) * 32,
        out=code % (slots + 1) * 32,
    )


def kernel(raw_lefts, raw_rights, has_left, has_right, has_sum, last, slots, first_group, segs, refs):
    refs = list(refs)
    first, turn_count, rights, lefts, outs = refs[:5]
    refs = refs[5:]
    left_raw, refs = refs[:raw_lefts], refs[raw_lefts:]
    right_raw, refs = refs[:raw_rights], refs[raw_rights:]
    panel, given, sum_in = None, [], None
    if has_left:
        panel, refs = refs[0], refs[1:]
    given, refs = refs[:has_right], refs[has_right:]
    if has_sum:
        sum_in, refs = refs[0], refs[1:]
    results, refs = refs[:2] if last else refs[:1], refs[2:] if last else refs[1:]
    if raw_lefts:
        panel, refs = refs[0], refs[1:]
    if raw_rights:
        weights, refs = refs[0], refs[1:]
    else:
        weights = given[0]
    flat, tall, sum_0, sum_1 = refs
    sums = (sum_0, sum_1)
    low = lax.broadcasted_iota(jnp.int32, (32, 128), 1) < 64

    def spread(source):
        for high in range(0, source.shape[0], 8):
            for pair in range(32):
                flat[pl.ds(high * 32 + pair, 8, stride=32), :] = source[
                    high : high + 8, pair * 128 : pair * 128 + 128
                ]

    def split(value):
        top = value.astype(jnp.bfloat16)
        return top, (value - top.astype(jnp.float32)).astype(jnp.bfloat16)

    for index, source in enumerate(left_raw):
        spread(source)
        for block in range(16):
            top, rest = split(flat[block * 32 : block * 32 + 32, :])
            panel[pl.ds(index * 512 + block * 32, 32), 0:128] = top
            panel[pl.ds(index * 512 + block * 32, 32), 128:256] = rest
    for index, source in enumerate(right_raw):
        spread(source)
        for block in range(16):
            both = flat[block * 32 : block * 32 + 32, :]
            swapped = pltpu.roll(both, 64, 1)
            spot = block % 4 * 128
            tall[pl.ds(spot, 32, stride=2), :] = jnp.where(low, both, 0.0)
            tall[pl.ds(spot + 1, 32, stride=2), :] = jnp.where(low, swapped, 0.0)
            tall[pl.ds(spot + 64, 32, stride=2), :] = jnp.where(low, 0.0, swapped)
            tall[pl.ds(spot + 65, 32, stride=2), :] = jnp.where(low, 0.0, both)
            top, rest = split(tall[spot : spot + 128, :])
            weights[index * 16 + block, 0] = top
            weights[index * 16 + block, 1] = rest

    sum_1[...] = jnp.zeros_like(sum_1)
    if has_sum:
        sum_0[...] = sum_in[...]
    else:
        sum_0[...] = jnp.zeros_like(sum_0)

    zero = jnp.zeros((128, 128), jnp.bfloat16)
    limit = weights.shape[0] - 1
    most = panel.shape[0] - 32

    def issue(chunk, unit, total):
        right = jnp.clip(rights[chunk] - first_group, 0, limit)
        top, rest = weights[right, 0], weights[right, 1]
        pltpu.matmul_push_rhs(
            jnp.concatenate(
                [jnp.concatenate([top, rest], 1), jnp.concatenate([top, zero], 1)], 0
            ),
            0,
            unit,
        )
        rows = [
            panel[pl.ds(pl.multiple_of(jnp.minimum(lefts[chunk * CHUNK + task], most), 32), 32), :]
            for task in range(CHUNK)
        ]
        pltpu.matmul_acc_lhs(total, jnp.concatenate(rows, 0), load_staged_rhs=0)

    def drain(chunk, unit, total):
        product = pltpu.matmul_pop(total)
        product = product[:, :128] + product[:, 128:]
        for task in range(CHUNK):
            rows = pl.ds(pl.multiple_of(outs[chunk * CHUNK + task], 32), 32)
            sums[unit][rows, :] += product[task * 32 : task * 32 + 32]

    def work(*totals):
        begin, turns = first[segs[0]] * TURN, turn_count[segs[0]]
        for seg in segs[1:]:
            turns = turns + turn_count[seg]
        for unit in range(2):
            issue(begin + unit, unit, totals[unit])

        @pl.loop(0, turns)
        def _(turn):
            chunk = begin + turn * TURN
            for unit in range(2):
                issue(chunk + 2 + unit, unit, totals[2 + unit])
            for unit in range(2):
                drain(chunk + unit, unit, totals[unit])
            for unit in range(2):
                issue(chunk + 4 + unit, unit, totals[unit])
            for unit in range(2):
                drain(chunk + 2 + unit, unit, totals[2 + unit])

        for unit in range(2):
            pltpu.matmul_pop(totals[unit])

    pl.run_scoped(
        work,
        *[pltpu.ACC(unit)((CHUNK * 32, 256), jnp.float32) for _ in range(2) for unit in range(2)],
    )

    if not last:
        results[0][...] = sum_0[...] + sum_1[...]
        return
    sum_0[...] = sum_0[...] + sum_1[...]
    layer = lax.axis_index("depth")
    size = results[0].shape[0]
    layers = slots // size
    for index, result in enumerate(results):
        row = (layer * size if index == 0 else lax.rem(layer + 1, layers) * size) * 32
        for high in range(0, size, 8):
            for pair in range(32):
                result[high : high + 8, pair * 128 : pair * 128 + 128] = sum_0[
                    pl.ds(row + high * 32 + pair, 8, stride=32), :
                ]


def tile_sum(tasks, seg, seg_count, left_raw, right_raw, panel, given, sum_in, last, slots, width, first_group):
    f32, bf16 = jnp.float32, jnp.bfloat16
    plans = [tasks[name] for name in ("first", "turns", "rights", "left", "out")]
    args = [*plans, *left_raw, *right_raw]
    smem, vmem = pl.BlockSpec(memory_space=pltpu.SMEM), pl.BlockSpec(memory_space=pltpu.VMEM)
    extra = [v for v in [panel, *given, sum_in] if v is not None]
    in_specs = [smem] * 5 + [vmem] * (len(left_raw) + len(right_raw) + len(extra))
    sum_shape = ((slots + 1) * 32, 128)
    shapes = (
        [jax.ShapeDtypeStruct((OUT_DEV, width), f32)] * 2
        if last
        else [jax.ShapeDtypeStruct(sum_shape, f32)]
    )
    if left_raw:
        shapes.append(jax.ShapeDtypeStruct((len(left_raw) * 512, 256), bf16))
    if right_raw:
        shapes.append(jax.ShapeDtypeStruct((len(right_raw) * 16, 2, 128, 128), bf16))
    body = functools.partial(
        kernel,
        len(left_raw),
        len(right_raw),
        panel is not None,
        len(given),
        sum_in is not None,
        last,
        slots,
        first_group,
        tuple(range(seg, seg + seg_count)),
    )
    return pl.pallas_call(
        lambda *refs: body(refs),
        out_shape=shapes,
        in_specs=in_specs,
        out_specs=[vmem] * len(shapes),
        scratch_shapes=[
            pltpu.VMEM((512, 128), f32),
            pltpu.VMEM((512, 128), f32),
            pltpu.VMEM(sum_shape, f32),
            pltpu.VMEM(sum_shape, f32),
        ],
        compiler_params=pltpu.CompilerParams(vmem_limit_bytes=44 << 20),
    )(*args, *extra)


def local(
    density,
    square_left,
    square_right,
    square_out,
    square_count,
    cube_left,
    cube_right,
    cube_out,
    cube_count,
):
    per_dev, width = density.shape
    rows, cols, layers = (lax.axis_size(name) for name in ("row", "col", "depth"))
    row, col, layer = (lax.axis_index(name) for name in ("row", "col", "depth"))
    slots = layers * OUT_DEV
    tasks = square_left.shape[0]
    place = jnp.arange(tasks, dtype=jnp.int32)

    def moved_left(left):
        from_col = lax.rem(col - left // (layers * per_dev) + cols, cols)
        from_layer = lax.rem(layer - left // per_dev % layers + layers, layers)
        return from_col, (from_col * layers + from_layer) * per_dev + left % per_dev

    def moved_right(right):
        away = lax.rem(row - right // per_dev + rows, rows)
        order = jnp.where(
            2 * away <= rows - 1 + rows % 2, 2 * away - 1, jnp.minimum(2 * (rows - away), rows - 1)
        )
        return jnp.maximum(order, 0) * per_dev + right % per_dev

    column = [density]
    for _ in range((rows - 1) // 2):
        ahead, behind = (column[-2], column[-1]) if len(column) > 1 else (density, density)
        column += [ring(ahead, "row"), ring(behind, "row", -1)]
    across = ring_all(density, "col")
    if rows % 2 == 0:
        opposite = ring(column[-2] if rows > 2 else density, "row")
    lefts = [piece for value in across for piece in ring_all(value, "depth")]

    groups = rows * per_dev
    _, left = moved_left(square_left)
    key = jnp.where(place < square_count[0], moved_right(square_right), groups)
    chunks = -(-(tasks // CHUNK + groups + TURN * rows + TURN) // 16) * 16
    square_tasks = plan(key, left, square_out, groups, per_dev, slots, chunks)
    from_col, left = moved_left(cube_left)
    left = left - jnp.where(from_col == 0, 0, layers * per_dev)
    key = jnp.where(from_col == 0, 0, groups) + moved_right(cube_right)
    key = jnp.where(place < cube_count[0], key, 2 * groups)
    chunks = -(-(tasks // CHUNK + 2 * groups + TURN * 2 + TURN) // 16) * 16
    cube_tasks = plan(key, left, cube_out, 2 * groups, groups, slots, chunks)

    total, panel, first = tile_sum(
        square_tasks, 0, 1, lefts, column[:1], None, [], None, False, slots, width, 0
    )
    weights = [first]
    for seg in range(1, len(column), 2):
        last = rows % 2 == 1 and seg + 2 == rows
        *result, piece = tile_sum(
            square_tasks, seg, 2, [], column[seg : seg + 2], panel, [], total, last,
            slots, width, seg * per_dev,
        )
        total = result[0]
        weights.append(piece)
    if rows % 2 == 0:
        *result, piece = tile_sum(
            square_tasks, rows - 1, 1, [], [opposite], panel, [], total, True,
            slots, width, (rows - 1) * per_dev,
        )
        weights.append(piece)
    mine, other = result
    weights = jnp.concatenate(weights, axis=0)
    square = mine + ring(other, "depth")

    near = ring_all(square, "depth")
    far = ring_all(square, "col")[1:]
    total, _ = tile_sum(
        cube_tasks, 0, 1, near, [], None, [weights], None, False, slots, width, 0
    )
    total, *far = lax.optimization_barrier((total, *far))
    far = [piece for value in far for piece in ring_all(value, "depth")]
    mine, other, _ = tile_sum(
        cube_tasks, 1, 1, far, [], None, [weights], total, True, slots, width, groups
    )
    cube = mine + ring(other, "depth")
    return 3.0 * square - 2.0 * cube


def solution(mesh):
    return jax.shard_map(
        local,
        mesh=mesh,
        in_specs=(
            P(("groups", "row", "col", "depth"), None),
            P(("groups", "row", "col", "depth")),
            P(("groups", "row", "col", "depth")),
            P(("groups", "row", "col", "depth")),
            P(("groups", "row", "col", "depth")),
            P(("groups", "row", "col", "depth")),
            P(("groups", "row", "col", "depth")),
            P(("groups", "row", "col", "depth")),
            P(("groups", "row", "col", "depth")),
        ),
        out_specs=P(("groups", "row", "col", "depth"), None),
        check_vma=False,
    )
```

```python
import functools
import math

import jax
import jax.numpy as jnp
from jax import lax
from jax.experimental import pallas as pl
from jax.experimental.pallas import tpu as pltpu
from jax.sharding import PartitionSpec as P

OUT_DEV = 16
CHUNK = 8
TURN = 4


def ring(value, axis, step=1):
    size = lax.axis_size(axis)
    return lax.ppermute(value, axis, [(i, (i + step) % size) for i in range(size)])


def ring_all(value, axis):
    pieces = [value]
    for _ in range(lax.axis_size(axis) - 1):
        pieces.append(ring(pieces[-1], axis))
    return pieces


def plan(key, left, out, groups, seg_groups, slots, chunks):
    tasks = key.shape[0]
    place = jnp.arange(tasks, dtype=jnp.int32)
    group = jnp.arange(groups, dtype=jnp.int32)
    segs = groups // seg_groups
    same = (key[:, None] == key[None, :]) & (place[:, None] < place[None, :])
    rank = jnp.sum(same.astype(jnp.int32), axis=0)
    count = jnp.sum((key[:, None] == group[None, :]).astype(jnp.int32), axis=0)
    filled = (count + CHUNK - 1) // CHUNK
    seg_id = group // seg_groups
    earlier = (group[:, None] < group[None, :]) & (seg_id[:, None] == seg_id[None, :])
    within = jnp.sum(jnp.where(earlier, filled[:, None], 0), axis=0)
    total = jnp.sum(filled.reshape(segs, seg_groups), axis=1)
    turns = (total + TURN - 1) // TURN
    seg = jnp.arange(segs, dtype=jnp.int32)
    first = jnp.sum(jnp.where(seg[:, None] < seg[None, :], turns[:, None], 0), axis=0)
    base = within + TURN * jnp.sum(
        jnp.where(seg_id[:, None] == seg[None, :], first[None, :], 0), axis=1
    )
    start = jnp.sum(jnp.where(key[:, None] == group[None, :], base[None, :] * CHUNK, 0), axis=1)
    position = jnp.where(key < groups, start + rank, -1)
    slot = jnp.arange(chunks * CHUNK, dtype=jnp.int32)
    code = jnp.sum(
        jnp.where(
            position[:, None] == slot[None, :], (left * (slots + 1) + out - slots)[:, None], 0
        ),
        axis=0,
    ) + slots
    chunk = jnp.arange(chunks, dtype=jnp.int32)
    rights = jnp.sum((base + filled)[:, None] <= chunk[None, :], axis=0, dtype=jnp.int32)
    return dict(
        first=first,
        turns=turns,
        rights=rights,
        left=code // (slots + 1) * 32,
        out=code % (slots + 1) * 32,
    )


def spread(source, flat):
    for high in range(0, source.shape[0], 8):
        for pair in range(32):
            flat[pl.ds(high * 32 + pair, 8, stride=32), :] = source[
                high : high + 8, pair * 128 : pair * 128 + 128
            ]


def split(value):
    top = value.astype(jnp.bfloat16)
    return top, (value - top.astype(jnp.float32)).astype(jnp.bfloat16)


def fill_panel(sources, panel, first, flat):
    for index, source in enumerate(sources):
        spread(source, flat)
        for block in range(16):
            rows = pl.ds((first + index) * 512 + block * 32, 32)
            top, rest = split(flat[block * 32 : block * 32 + 32, :])
            panel[rows, 0:128] = top
            panel[rows, 128:256] = rest


def fill_weights(sources, weights, flat, tall):
    low = lax.broadcasted_iota(jnp.int32, (32, 128), 1) < 64
    for index, source in enumerate(sources):
        spread(source, flat)
        for block in range(16):
            both = flat[block * 32 : block * 32 + 32, :]
            swapped = pltpu.roll(both, 64, 1)
            spot = block % 4 * 128
            tall[pl.ds(spot, 32, stride=2), :] = jnp.where(low, both, 0.0)
            tall[pl.ds(spot + 1, 32, stride=2), :] = jnp.where(low, swapped, 0.0)
            tall[pl.ds(spot + 64, 32, stride=2), :] = jnp.where(low, 0.0, swapped)
            tall[pl.ds(spot + 65, 32, stride=2), :] = jnp.where(low, 0.0, both)
            top, rest = split(tall[spot : spot + 128, :])
            weights[index * 16 + block, 0] = top
            weights[index * 16 + block, 1] = rest


def prepare_kernel(raw_lefts, *refs):
    sources, (panel, weights, flat, tall) = refs[:-4], refs[-4:]
    fill_panel(sources[:raw_lefts], panel, 0, flat)
    fill_weights(sources[raw_lefts:], weights, flat, tall)


def prepare(lefts, rights):
    vmem = pl.BlockSpec(memory_space=pltpu.VMEM)
    return pl.pallas_call(
        functools.partial(prepare_kernel, len(lefts)),
        out_shape=[
            jax.ShapeDtypeStruct((len(lefts) * 512, 256), jnp.bfloat16),
            jax.ShapeDtypeStruct((len(rights) * 16, 2, 128, 128), jnp.bfloat16),
        ],
        in_specs=[vmem] * (len(lefts) + len(rights)),
        out_specs=[vmem] * 2,
        scratch_shapes=[pltpu.VMEM((512, 128), jnp.float32)] * 2,
        compiler_params=pltpu.CompilerParams(vmem_limit_bytes=44 << 20),
    )(*lefts, *rights)


def kernel(raw_lefts, raw_rights, has_left, has_right, has_sum, last, slots, first_group, segs, keep, refs):
    refs = list(refs)
    first, turn_count, rights, lefts, outs = refs[:5]
    refs = refs[5:]
    left_raw, refs = refs[:raw_lefts], refs[raw_lefts:]
    right_raw, refs = refs[:raw_rights], refs[raw_rights:]
    panel, given, sum_in = None, [], None
    if has_left:
        panel, refs = refs[0], refs[1:]
    given, refs = refs[:has_right], refs[has_right:]
    if has_sum:
        sum_in, refs = refs[0], refs[1:]
    results, refs = refs[:2] if last else refs[:1], refs[2:] if last else refs[1:]
    flat, tall, sum_0, sum_1 = refs[-4:]
    start = 0
    if raw_lefts:
        whole, refs = refs[0], refs[1:]
        if has_left:
            start = panel.shape[0] // 512
            whole[: panel.shape[0], :] = panel[...]
        panel = whole
    weights = refs[0] if raw_rights else given[0]
    sums = (sum_0, sum_1)
    fill_panel(left_raw, panel, start, flat)
    fill_weights(right_raw, weights, flat, tall)

    sum_1[...] = jnp.zeros_like(sum_1)
    if has_sum:
        sum_0[...] = sum_in[...]
    else:
        sum_0[...] = jnp.zeros_like(sum_0)

    zero = jnp.zeros((128, 128), jnp.bfloat16)
    limit = weights.shape[0] - 1
    most = panel.shape[0] - 32

    def issue(chunk, unit, total):
        right = jnp.clip(rights[chunk] - first_group, 0, limit)
        top, rest = weights[right, 0], weights[right, 1]
        pltpu.matmul_push_rhs(
            jnp.concatenate(
                [jnp.concatenate([top, rest], 1), jnp.concatenate([top, zero], 1)], 0
            ),
            0,
            unit,
        )
        rows = [
            panel[pl.ds(pl.multiple_of(jnp.minimum(lefts[chunk * CHUNK + task], most), 32), 32), :]
            for task in range(CHUNK)
        ]
        pltpu.matmul_acc_lhs(total, jnp.concatenate(rows, 0), load_staged_rhs=0)

    def drain(chunk, unit, total):
        product = pltpu.matmul_pop(total)
        product = product[:, :128] + product[:, 128:]
        for task in range(CHUNK):
            rows = pl.ds(pl.multiple_of(outs[chunk * CHUNK + task], 32), 32)
            sums[unit][rows, :] += product[task * 32 : task * 32 + 32]

    def work(*totals):
        begin, turns = first[segs[0]] * TURN, turn_count[segs[0]]
        for seg in segs[1:]:
            turns = turns + turn_count[seg]
        for unit in range(2):
            issue(begin + unit, unit, totals[unit])

        @pl.loop(0, turns)
        def _(turn):
            chunk = begin + turn * TURN
            for unit in range(2):
                issue(chunk + 2 + unit, unit, totals[2 + unit])
            for unit in range(2):
                drain(chunk + unit, unit, totals[unit])
            for unit in range(2):
                issue(chunk + 4 + unit, unit, totals[unit])
            for unit in range(2):
                drain(chunk + 2 + unit, unit, totals[2 + unit])

        for unit in range(2):
            pltpu.matmul_pop(totals[unit])

    pl.run_scoped(
        work,
        *[pltpu.ACC(unit)((CHUNK * 32, 256), jnp.float32) for _ in range(2) for unit in range(2)],
    )

    if not last:
        results[0][...] = sum_0[...] + sum_1[...]
        return
    sum_0[...] = sum_0[...] + sum_1[...]
    layer = lax.axis_index("depth")
    size = results[0].shape[0]
    layers = slots // size
    for index, result in enumerate(results):
        row = (layer * size if index == 0 else lax.rem(layer + 1, layers) * size) * 32
        for high in range(0, size, 8):
            for pair in range(32):
                result[high : high + 8, pair * 128 : pair * 128 + 128] = sum_0[
                    pl.ds(row + high * 32 + pair, 8, stride=32), :
                ]


def tile_sum(tasks, seg, seg_count, left_raw, right_raw, panel, given, sum_in, last, slots, width, first_group, keep=False):
    f32, bf16 = jnp.float32, jnp.bfloat16
    plans = [tasks[name] for name in ("first", "turns", "rights", "left", "out")]
    args = [*plans, *left_raw, *right_raw]
    smem, vmem = pl.BlockSpec(memory_space=pltpu.SMEM), pl.BlockSpec(memory_space=pltpu.VMEM)
    extra = [v for v in [panel, *given, sum_in] if v is not None]
    in_specs = [smem] * 5 + [vmem] * (len(left_raw) + len(right_raw) + len(extra))
    sum_shape = ((slots + 1) * 32, 128)
    shapes = (
        [jax.ShapeDtypeStruct((OUT_DEV, width), f32)] * 2
        if last
        else [jax.ShapeDtypeStruct(sum_shape, f32)]
    )
    blocks = len(left_raw) * 512 + (0 if panel is None else panel.shape[0])
    scratch = []
    if left_raw and keep:
        shapes.append(jax.ShapeDtypeStruct((blocks, 256), bf16))
    elif left_raw:
        scratch = [pltpu.VMEM((blocks, 256), bf16)]
    if right_raw:
        shapes.append(jax.ShapeDtypeStruct((len(right_raw) * 16, 2, 128, 128), bf16))
    body = functools.partial(
        kernel,
        len(left_raw),
        len(right_raw),
        panel is not None,
        len(given),
        sum_in is not None,
        last,
        slots,
        first_group,
        tuple(range(seg, seg + seg_count)),
        keep,
    )
    return pl.pallas_call(
        lambda *refs: body(refs),
        out_shape=shapes,
        in_specs=in_specs,
        out_specs=[vmem] * len(shapes),
        scratch_shapes=[
            *scratch,
            pltpu.VMEM((512, 128), f32),
            pltpu.VMEM((512, 128), f32),
            pltpu.VMEM(sum_shape, f32),
            pltpu.VMEM(sum_shape, f32),
        ],
        compiler_params=pltpu.CompilerParams(vmem_limit_bytes=44 << 20),
    )(*args, *extra)


def local(
    density,
    square_left,
    square_right,
    square_out,
    square_count,
    cube_left,
    cube_right,
    cube_out,
    cube_count,
):
    per_dev, width = density.shape
    rows, cols, layers = (lax.axis_size(name) for name in ("row", "col", "depth"))
    row, col, layer = (lax.axis_index(name) for name in ("row", "col", "depth"))
    slots = layers * OUT_DEV
    tasks = square_left.shape[0]
    place = jnp.arange(tasks, dtype=jnp.int32)

    def moved_left(left):
        from_col = lax.rem(col - left // (layers * per_dev) + cols, cols)
        from_layer = lax.rem(layer - left // per_dev % layers + layers, layers)
        return from_col, (from_col * layers + from_layer) * per_dev + left % per_dev

    def moved_right(right):
        away = lax.rem(row - right // per_dev + rows, rows)
        order = jnp.where(
            2 * away <= rows - 1 + rows % 2, 2 * away - 1, jnp.minimum(2 * (rows - away), rows - 1)
        )
        return jnp.maximum(order, 0) * per_dev + right % per_dev

    column = [density]
    for _ in range((rows - 1) // 2):
        ahead, behind = (column[-2], column[-1]) if len(column) > 1 else (density, density)
        column += [ring(ahead, "row"), ring(behind, "row", -1)]
    across = ring_all(density, "col")
    lefts = [piece for value in across for piece in ring_all(value, "depth")]

    groups = rows * per_dev
    _, left = moved_left(square_left)
    key = jnp.where(place < square_count[0], moved_right(square_right), groups)
    chunks = -(-(tasks // CHUNK + groups + TURN * rows + TURN) // 16) * 16
    square_tasks = plan(key, left, square_out, groups, per_dev, slots, chunks)
    from_col, left = moved_left(cube_left)
    left = left - jnp.where(from_col == 0, 0, layers * per_dev)
    key = jnp.where(from_col == 0, 0, groups) + moved_right(cube_right)
    key = jnp.where(place < cube_count[0], key, 2 * groups)
    chunks = -(-(tasks // CHUNK + 2 * groups + TURN * 2 + TURN) // 16) * 16
    cube_tasks = plan(key, left, cube_out, 2 * groups, groups, slots, chunks)

    panel, first = prepare(lefts[:layers], column[:1])
    total, panel = tile_sum(
        square_tasks, 0, 1, lefts[layers:], [], panel, [first], None, False, slots, width, 0, True
    )
    weights = [first]
    if rows % 2 == 0:
        column[-2], total = lax.optimization_barrier((column[-2], total))
        opposite = ring(column[-2] if rows > 2 else density, "row")
    for seg in range(1, len(column), 2):
        last = rows % 2 == 1 and seg + 2 == rows
        *result, piece = tile_sum(
            square_tasks, seg, 2, [], column[seg : seg + 2], panel, [], total, last,
            slots, width, seg * per_dev,
        )
        total = result[0]
        weights.append(piece)
    if rows % 2 == 0:
        *result, piece = tile_sum(
            square_tasks, rows - 1, 1, [], [opposite], panel, [], total, True,
            slots, width, (rows - 1) * per_dev,
        )
        weights.append(piece)
    mine, other = result
    weights = jnp.concatenate(weights, axis=0)
    square = mine + ring(other, "depth")

    near = ring_all(square, "depth")
    far = ring_all(square, "col")[1:]
    (total,) = tile_sum(
        cube_tasks, 0, 1, near, [], None, [weights], None, False, slots, width, 0
    )
    total, *far = lax.optimization_barrier((total, *far))
    far = [piece for value in far for piece in ring_all(value, "depth")]
    mine, other = tile_sum(
        cube_tasks, 1, 1, far, [], None, [weights], total, True, slots, width, groups
    )
    cube = mine + ring(other, "depth")
    return 3.0 * square - 2.0 * cube


def solution(mesh):
    return jax.shard_map(
        local,
        mesh=mesh,
        in_specs=(
            P(("groups", "row", "col", "depth"), None),
            P(("groups", "row", "col", "depth")),
            P(("groups", "row", "col", "depth")),
            P(("groups", "row", "col", "depth")),
            P(("groups", "row", "col", "depth")),
            P(("groups", "row", "col", "depth")),
            P(("groups", "row", "col", "depth")),
            P(("groups", "row", "col", "depth")),
            P(("groups", "row", "col", "depth")),
        ),
        out_specs=P(("groups", "row", "col", "depth"), None),
        check_vma=False,
    )
```

```python
import functools
import math

import jax
import jax.numpy as jnp
from jax import lax
from jax.experimental import pallas as pl
from jax.experimental.pallas import tpu as pltpu
from jax.sharding import PartitionSpec as P

OUT_DEV = 16
CHUNK = 8
TURN = 8


def ring(value, axis, step=1):
    size = lax.axis_size(axis)
    return lax.ppermute(value, axis, [(i, (i + step) % size) for i in range(size)])


def ring_all(value, axis):
    pieces = [value]
    for _ in range(lax.axis_size(axis) - 1):
        pieces.append(ring(pieces[-1], axis))
    return pieces


def plan(key, left, out, groups, seg_groups, slots, chunks):
    tasks = key.shape[0]
    place = jnp.arange(tasks, dtype=jnp.int32)
    group = jnp.arange(groups, dtype=jnp.int32)
    segs = groups // seg_groups
    same = (key[:, None] == key[None, :]) & (place[:, None] < place[None, :])
    rank = jnp.sum(same.astype(jnp.int32), axis=0)
    count = jnp.sum((key[:, None] == group[None, :]).astype(jnp.int32), axis=0)
    filled = (count + CHUNK - 1) // CHUNK
    seg_id = group // seg_groups
    earlier = (group[:, None] < group[None, :]) & (seg_id[:, None] == seg_id[None, :])
    within = jnp.sum(jnp.where(earlier, filled[:, None], 0), axis=0)
    total = jnp.sum(filled.reshape(segs, seg_groups), axis=1)
    turns = (total + TURN - 1) // TURN
    seg = jnp.arange(segs, dtype=jnp.int32)
    first = jnp.sum(jnp.where(seg[:, None] < seg[None, :], turns[:, None], 0), axis=0)
    base = within + TURN * jnp.sum(
        jnp.where(seg_id[:, None] == seg[None, :], first[None, :], 0), axis=1
    )
    start = jnp.sum(jnp.where(key[:, None] == group[None, :], base[None, :] * CHUNK, 0), axis=1)
    position = jnp.where(key < groups, start + rank, -1)
    slot = jnp.arange(chunks * CHUNK, dtype=jnp.int32)
    code = jnp.sum(
        jnp.where(
            position[:, None] == slot[None, :], (left * (slots + 1) + out - slots)[:, None], 0
        ),
        axis=0,
    ) + slots
    chunk = jnp.arange(chunks, dtype=jnp.int32)
    rights = jnp.sum((base + filled)[:, None] <= chunk[None, :], axis=0, dtype=jnp.int32)
    return dict(
        first=first,
        turns=turns,
        rights=rights,
        left=code // (slots + 1) * 64,
        out=code % (slots + 1) * 64,
    )


def spread(source, flat):
    for high in range(0, source.shape[0], 8):
        for pair in range(32):
            flat[pl.ds(high * 32 + pair, 8, stride=32), :] = source[
                high : high + 8, pair * 128 : pair * 128 + 128
            ]


def low_half(rows):
    return lax.broadcasted_iota(jnp.int32, (rows, 128), 1) < 64


def split(value):
    top = value.astype(jnp.bfloat16).astype(jnp.float32)
    return top, value - top


def fill_panel(sources, panel, first, flat):
    low = low_half(32)
    for index, source in enumerate(sources):
        spread(source, flat)
        for block in range(16):
            row = (first + index) * 1024 + block * 64
            top, rest = split(flat[block * 32 : block * 32 + 32, :])
            even = jnp.where(low, top, pltpu.roll(rest, 64, 1))
            odd = jnp.where(low, pltpu.roll(top, 64, 1), rest)
            panel[pl.ds(row, 32), :] = even.astype(jnp.bfloat16)
            panel[pl.ds(row + 32, 32), :] = odd.astype(jnp.bfloat16)


def fill_weights(sources, weights, flat, tall):
    low, low_tall = low_half(32), low_half(64)
    for index, source in enumerate(sources):
        spread(source, flat)
        for block in range(16):
            both = flat[block * 32 : block * 32 + 32, :]
            swapped = pltpu.roll(both, 64, 1)
            spot = block % 4 * 64
            tall[pl.ds(spot, 32, stride=2), :] = jnp.where(low, both, swapped)
            tall[pl.ds(spot + 1, 32, stride=2), :] = jnp.where(low, swapped, both)
            top, rest = split(tall[spot : spot + 64, :])
            weights[index * 16 + block, 0:64] = jnp.where(low_tall, top, rest).astype(jnp.bfloat16)
            weights[index * 16 + block, 64:128] = jnp.where(low_tall, top, 0.0).astype(jnp.bfloat16)


def prepare_kernel(raw_lefts, *refs):
    sources, (panel, weights, flat, tall) = refs[:-4], refs[-4:]
    fill_panel(sources[:raw_lefts], panel, 0, flat)
    fill_weights(sources[raw_lefts:], weights, flat, tall)


def prepare(lefts, rights):
    vmem = pl.BlockSpec(memory_space=pltpu.VMEM)
    return pl.pallas_call(
        functools.partial(prepare_kernel, len(lefts)),
        out_shape=[
            jax.ShapeDtypeStruct((len(lefts) * 1024, 128), jnp.bfloat16),
            jax.ShapeDtypeStruct((len(rights) * 16, 128, 128), jnp.bfloat16),
        ],
        in_specs=[vmem] * (len(lefts) + len(rights)),
        out_specs=[vmem] * 2,
        scratch_shapes=[pltpu.VMEM((size, 128), jnp.float32) for size in (512, 256)],
        compiler_params=pltpu.CompilerParams(vmem_limit_bytes=44 << 20),
    )(*lefts, *rights)


def kernel(raw_lefts, raw_rights, has_left, has_right, has_sum, last, slots, first_group, segs, keep, refs):
    refs = list(refs)
    first, turn_count, rights, lefts, outs = refs[:5]
    refs = refs[5:]
    left_raw, refs = refs[:raw_lefts], refs[raw_lefts:]
    right_raw, refs = refs[:raw_rights], refs[raw_rights:]
    panel, given, sum_in = None, [], None
    if has_left:
        panel, refs = refs[0], refs[1:]
    given, refs = refs[:has_right], refs[has_right:]
    if has_sum:
        sum_in, refs = refs[0], refs[1:]
    results, refs = refs[:2] if last else refs[:1], refs[2:] if last else refs[1:]
    flat, tall, folded, sum_0, sum_1 = refs[-5:]
    start = 0
    if raw_lefts:
        whole, refs = refs[0], refs[1:]
        if has_left:
            start = panel.shape[0] // 1024
            whole[: panel.shape[0], :] = panel[...]
        panel = whole
    weights = refs[0] if raw_rights else given[0]
    sums = (sum_0, sum_1)
    fill_panel(left_raw, panel, start, flat)
    fill_weights(right_raw, weights, flat, tall)

    sum_1[...] = jnp.zeros_like(sum_1)
    if has_sum:
        sum_0[...] = sum_in[...]
    else:
        sum_0[...] = jnp.zeros_like(sum_0)

    zero = jnp.zeros((128, 128), jnp.bfloat16)
    limit = weights.shape[0] - 1
    most = panel.shape[0] - 64

    def issue(chunk, unit, totals):
        first_right, second_right = (
            weights[jnp.clip(rights[chunk + side] - first_group, 0, limit)] for side in range(2)
        )
        pltpu.matmul_push_rhs(
            jnp.concatenate(
                [
                    jnp.concatenate([first_right, zero], 1),
                    jnp.concatenate([zero, second_right], 1),
                ],
                0,
            ),
            0,
            unit,
        )
        for task, total in enumerate(totals):
            sides = []
            for side in range(2):
                row = jnp.minimum(lefts[(chunk + side) * CHUNK + task], most)
                sides.append(panel[pl.ds(pl.multiple_of(row, 64), 64), :])
            pltpu.matmul_acc_lhs(
                total, jnp.concatenate(sides, 1), load_staged_rhs=0 if task == 0 else None
            )

    def drain(chunk, unit, totals):
        for task, total in enumerate(totals):
            product = pltpu.matmul_pop(total)
            for side in range(2):
                row = outs[(chunk + side) * CHUNK + task]
                rows = pl.ds(pl.multiple_of(row, 64), 64)
                sums[unit][rows, :] += product[:, side * 128 : side * 128 + 128]

    def work(*totals):
        totals = [totals[index : index + CHUNK] for index in range(0, len(totals), CHUNK)]
        begin, turns = first[segs[0]] * TURN, turn_count[segs[0]]
        for seg in segs[1:]:
            turns = turns + turn_count[seg]
        for unit in range(2):
            issue(begin + 2 * unit, unit, totals[unit])

        @pl.loop(0, turns)
        def _(turn):
            chunk = begin + turn * TURN
            for unit in range(2):
                issue(chunk + 4 + 2 * unit, unit, totals[2 + unit])
            for unit in range(2):
                drain(chunk + 2 * unit, unit, totals[unit])
            for unit in range(2):
                issue(chunk + 8 + 2 * unit, unit, totals[unit])
            for unit in range(2):
                drain(chunk + 4 + 2 * unit, unit, totals[2 + unit])

        for unit in range(2):
            for total in totals[unit]:
                pltpu.matmul_pop(total)

    pl.run_scoped(
        work,
        *[
            pltpu.ACC(unit)((64, 256), jnp.float32)
            for _ in range(2)
            for unit in range(2)
            for _ in range(CHUNK)
        ],
    )

    if not last:
        results[0][...] = sum_0[...] + sum_1[...]
        return
    low = low_half(32)
    for block in range(slots):
        rows = pl.ds(block * 64, 64)
        value = sum_0[rows, :] + sum_1[rows, :]
        value = value + pltpu.roll(value, 64, 1)
        folded[pl.ds(block * 32, 32), :] = jnp.where(low, value[:32], value[32:])
    layer = lax.axis_index("depth")
    size = results[0].shape[0]
    layers = slots // size
    for index, result in enumerate(results):
        row = (layer * size if index == 0 else lax.rem(layer + 1, layers) * size) * 32
        for high in range(0, size, 8):
            for pair in range(32):
                result[high : high + 8, pair * 128 : pair * 128 + 128] = folded[
                    pl.ds(row + high * 32 + pair, 8, stride=32), :
                ]


def tile_sum(tasks, seg, seg_count, left_raw, right_raw, panel, given, sum_in, last, slots, width, first_group, keep=False):
    f32, bf16 = jnp.float32, jnp.bfloat16
    plans = [tasks[name] for name in ("first", "turns", "rights", "left", "out")]
    args = [*plans, *left_raw, *right_raw]
    smem, vmem = pl.BlockSpec(memory_space=pltpu.SMEM), pl.BlockSpec(memory_space=pltpu.VMEM)
    extra = [v for v in [panel, *given, sum_in] if v is not None]
    in_specs = [smem] * 5 + [vmem] * (len(left_raw) + len(right_raw) + len(extra))
    sum_shape = ((slots + 1) * 64, 128)
    shapes = (
        [jax.ShapeDtypeStruct((OUT_DEV, width), f32)] * 2
        if last
        else [jax.ShapeDtypeStruct(sum_shape, f32)]
    )
    blocks = len(left_raw) * 1024 + (0 if panel is None else panel.shape[0])
    scratch = []
    if left_raw and keep:
        shapes.append(jax.ShapeDtypeStruct((blocks, 128), bf16))
    elif left_raw:
        scratch = [pltpu.VMEM((blocks, 128), bf16)]
    if right_raw:
        shapes.append(jax.ShapeDtypeStruct((len(right_raw) * 16, 128, 128), bf16))
    body = functools.partial(
        kernel,
        len(left_raw),
        len(right_raw),
        panel is not None,
        len(given),
        sum_in is not None,
        last,
        slots,
        first_group,
        tuple(range(seg, seg + seg_count)),
        keep,
    )
    return pl.pallas_call(
        lambda *refs: body(refs),
        out_shape=shapes,
        in_specs=in_specs,
        out_specs=[vmem] * len(shapes),
        scratch_shapes=[
            *scratch,
            pltpu.VMEM((512, 128), f32),
            pltpu.VMEM((256, 128), f32),
            pltpu.VMEM((slots * 32 if last else 8, 128), f32),
            pltpu.VMEM(sum_shape, f32),
            pltpu.VMEM(sum_shape, f32),
        ],
        compiler_params=pltpu.CompilerParams(vmem_limit_bytes=44 << 20),
    )(*args, *extra)


def local(
    density,
    square_left,
    square_right,
    square_out,
    square_count,
    cube_left,
    cube_right,
    cube_out,
    cube_count,
):
    per_dev, width = density.shape
    rows, cols, layers = (lax.axis_size(name) for name in ("row", "col", "depth"))
    row, col, layer = (lax.axis_index(name) for name in ("row", "col", "depth"))
    slots = layers * OUT_DEV
    tasks = square_left.shape[0]
    place = jnp.arange(tasks, dtype=jnp.int32)

    def moved_left(left):
        from_col = lax.rem(col - left // (layers * per_dev) + cols, cols)
        from_layer = lax.rem(layer - left // per_dev % layers + layers, layers)
        return from_col, (from_col * layers + from_layer) * per_dev + left % per_dev

    def moved_right(right):
        away = lax.rem(row - right // per_dev + rows, rows)
        order = jnp.where(
            2 * away <= rows - 1 + rows % 2, 2 * away - 1, jnp.minimum(2 * (rows - away), rows - 1)
        )
        return jnp.maximum(order, 0) * per_dev + right % per_dev

    column = [density]
    for _ in range((rows - 1) // 2):
        ahead, behind = (column[-2], column[-1]) if len(column) > 1 else (density, density)
        column += [ring(ahead, "row"), ring(behind, "row", -1)]
    across = ring_all(density, "col")
    lefts = [piece for value in across for piece in ring_all(value, "depth")]

    groups = rows * per_dev
    _, left = moved_left(square_left)
    key = jnp.where(place < square_count[0], moved_right(square_right), groups)
    chunks = -(-(tasks // CHUNK + groups + TURN * rows + TURN) // 16) * 16
    square_tasks = plan(key, left, square_out, groups, per_dev, slots, chunks)
    from_col, left = moved_left(cube_left)
    left = left - jnp.where(from_col == 0, 0, layers * per_dev)
    key = jnp.where(from_col == 0, 0, groups) + moved_right(cube_right)
    key = jnp.where(place < cube_count[0], key, 2 * groups)
    chunks = -(-(tasks // CHUNK + 2 * groups + TURN * 2 + TURN) // 16) * 16
    cube_tasks = plan(key, left, cube_out, 2 * groups, groups, slots, chunks)

    panel, first = prepare(lefts[:layers], column[:1])
    total, panel = tile_sum(
        square_tasks, 0, 1, lefts[layers:], [], panel, [first], None, False, slots, width, 0, True
    )
    weights = [first]
    if rows % 2 == 0:
        column[-2], total = lax.optimization_barrier((column[-2], total))
        opposite = ring(column[-2] if rows > 2 else density, "row")
    for seg in range(1, len(column), 2):
        last = rows % 2 == 1 and seg + 2 == rows
        *result, piece = tile_sum(
            square_tasks, seg, 2, [], column[seg : seg + 2], panel, [], total, last,
            slots, width, seg * per_dev,
        )
        total = result[0]
        weights.append(piece)
    if rows % 2 == 0:
        *result, piece = tile_sum(
            square_tasks, rows - 1, 1, [], [opposite], panel, [], total, True,
            slots, width, (rows - 1) * per_dev,
        )
        weights.append(piece)
    mine, other = result
    weights = jnp.concatenate(weights, axis=0)
    square = mine + ring(other, "depth")

    near = ring_all(square, "depth")
    far = ring_all(square, "col")[1:]
    (total,) = tile_sum(
        cube_tasks, 0, 1, near, [], None, [weights], None, False, slots, width, 0
    )
    total, *far = lax.optimization_barrier((total, *far))
    far = [piece for value in far for piece in ring_all(value, "depth")]
    mine, other = tile_sum(
        cube_tasks, 1, 1, far, [], None, [weights], total, True, slots, width, groups
    )
    cube = mine + ring(other, "depth")
    return 3.0 * square - 2.0 * cube


def solution(mesh):
    return jax.shard_map(
        local,
        mesh=mesh,
        in_specs=(
            P(("groups", "row", "col", "depth"), None),
            P(("groups", "row", "col", "depth")),
            P(("groups", "row", "col", "depth")),
            P(("groups", "row", "col", "depth")),
            P(("groups", "row", "col", "depth")),
            P(("groups", "row", "col", "depth")),
            P(("groups", "row", "col", "depth")),
            P(("groups", "row", "col", "depth")),
            P(("groups", "row", "col", "depth")),
        ),
        out_specs=P(("groups", "row", "col", "depth"), None),
        check_vma=False,
    )
```

```python
import functools
import math

import jax
import jax.numpy as jnp
from jax import lax
from jax.experimental import pallas as pl
from jax.experimental.pallas import tpu as pltpu
from jax.sharding import PartitionSpec as P

OUT_DEV = 16
CHUNK = 8
TURN = 8


def ring(value, axis, step=1):
    size = lax.axis_size(axis)
    return lax.ppermute(value, axis, [(i, (i + step) % size) for i in range(size)])


def ring_all(value, axis):
    pieces = [value]
    for _ in range(lax.axis_size(axis) - 1):
        pieces.append(ring(pieces[-1], axis))
    return pieces


def plan(key, left, out, groups, seg_groups, slots, chunks):
    tasks = key.shape[0]
    place = jnp.arange(tasks, dtype=jnp.int32)
    group = jnp.arange(groups, dtype=jnp.int32)
    segs = groups // seg_groups
    same = (key[:, None] == key[None, :]) & (place[:, None] < place[None, :])
    rank = jnp.sum(same.astype(jnp.int32), axis=0)
    count = jnp.sum((key[:, None] == group[None, :]).astype(jnp.int32), axis=0)
    filled = (count + CHUNK - 1) // CHUNK
    seg_id = group // seg_groups
    earlier = (group[:, None] < group[None, :]) & (seg_id[:, None] == seg_id[None, :])
    within = jnp.sum(jnp.where(earlier, filled[:, None], 0), axis=0)
    total = jnp.sum(filled.reshape(segs, seg_groups), axis=1)
    turns = (total + TURN - 1) // TURN
    seg = jnp.arange(segs, dtype=jnp.int32)
    first = jnp.sum(jnp.where(seg[:, None] < seg[None, :], turns[:, None], 0), axis=0)
    base = within + TURN * jnp.sum(
        jnp.where(seg_id[:, None] == seg[None, :], first[None, :], 0), axis=1
    )
    start = jnp.sum(jnp.where(key[:, None] == group[None, :], base[None, :] * CHUNK, 0), axis=1)
    position = jnp.where(key < groups, start + rank, -1)
    slot = jnp.arange(chunks * CHUNK, dtype=jnp.int32)
    code = jnp.sum(
        jnp.where(
            position[:, None] == slot[None, :], (left * (slots + 1) + out - slots)[:, None], 0
        ),
        axis=0,
    ) + slots
    chunk = jnp.arange(chunks, dtype=jnp.int32)
    rights = jnp.sum((base + filled)[:, None] <= chunk[None, :], axis=0, dtype=jnp.int32)
    return dict(
        first=first,
        turns=turns,
        rights=rights,
        left=code // (slots + 1) * 64,
        out=code % (slots + 1) * 64,
    )


def spread(source, flat):
    for high in range(0, source.shape[0], 8):
        for pair in range(32):
            flat[pl.ds(high * 32 + pair, 8, stride=32), :] = source[
                high : high + 8, pair * 128 : pair * 128 + 128
            ]


def low_half(rows):
    return lax.broadcasted_iota(jnp.int32, (rows, 128), 1) < 64


def split(value):
    top = value.astype(jnp.bfloat16).astype(jnp.float32)
    return top, value - top


def fill_panel(sources, panel, first, flat):
    low = low_half(32)
    for index, source in enumerate(sources):
        spread(source, flat)
        for block in range(16):
            row = (first + index) * 1024 + block * 64
            top, rest = split(flat[block * 32 : block * 32 + 32, :])
            even = jnp.where(low, top, pltpu.roll(rest, 64, 1))
            odd = jnp.where(low, pltpu.roll(top, 64, 1), rest)
            panel[pl.ds(row, 32), :] = even.astype(jnp.bfloat16)
            panel[pl.ds(row + 32, 32), :] = odd.astype(jnp.bfloat16)


def fill_weights(sources, weights, flat, tall):
    low, low_tall = low_half(32), low_half(64)
    for index, source in enumerate(sources):
        spread(source, flat)
        for block in range(16):
            both = flat[block * 32 : block * 32 + 32, :]
            swapped = pltpu.roll(both, 64, 1)
            spot = block % 4 * 64
            tall[pl.ds(spot, 32, stride=2), :] = jnp.where(low, both, swapped)
            tall[pl.ds(spot + 1, 32, stride=2), :] = jnp.where(low, swapped, both)
            top, rest = split(tall[spot : spot + 64, :])
            weights[index * 16 + block, 0:64] = jnp.where(low_tall, top, rest).astype(jnp.bfloat16)
            weights[index * 16 + block, 64:128] = jnp.where(low_tall, top, 0.0).astype(jnp.bfloat16)


def prepare_kernel(raw_lefts, *refs):
    sources, (panel, weights, flat, tall) = refs[:-4], refs[-4:]
    fill_panel(sources[:raw_lefts], panel, 0, flat)
    fill_weights(sources[raw_lefts:], weights, flat, tall)


def prepare(lefts, rights):
    vmem = pl.BlockSpec(memory_space=pltpu.VMEM)
    return pl.pallas_call(
        functools.partial(prepare_kernel, len(lefts)),
        out_shape=[
            jax.ShapeDtypeStruct((len(lefts) * 1024, 128), jnp.bfloat16),
            jax.ShapeDtypeStruct((len(rights) * 16, 128, 128), jnp.bfloat16),
        ],
        in_specs=[vmem] * (len(lefts) + len(rights)),
        out_specs=[vmem] * 2,
        scratch_shapes=[pltpu.VMEM((size, 128), jnp.float32) for size in (512, 256)],
        compiler_params=pltpu.CompilerParams(vmem_limit_bytes=44 << 20),
    )(*lefts, *rights)


def kernel(raw_lefts, raw_rights, has_left, has_right, has_sum, last, slots, first_group, segs, keep, refs):
    refs = list(refs)
    first, turn_count, rights, lefts, outs = refs[:5]
    refs = refs[5:]
    left_raw, refs = refs[:raw_lefts], refs[raw_lefts:]
    right_raw, refs = refs[:raw_rights], refs[raw_rights:]
    panel, given, sum_in = None, [], None
    if has_left:
        panel, refs = refs[0], refs[1:]
    given, refs = refs[:has_right], refs[has_right:]
    if has_sum:
        sum_in, refs = refs[0], refs[1:]
    results, refs = refs[:2] if last else refs[:1], refs[2:] if last else refs[1:]
    flat, tall, folded, sum_0, sum_1 = refs[-5:]
    start = 0
    if raw_lefts:
        whole, refs = refs[0], refs[1:]
        if has_left:
            start = panel.shape[0] // 1024
            whole[: panel.shape[0], :] = panel[...]
        panel = whole
    weights = refs[0] if raw_rights else given[0]
    sums = (sum_0, sum_1)
    fill_panel(left_raw, panel, start, flat)
    fill_weights(right_raw, weights, flat, tall)

    sum_1[...] = jnp.zeros_like(sum_1)
    if has_sum:
        sum_0[...] = sum_in[...]
    else:
        sum_0[...] = jnp.zeros_like(sum_0)

    zero = jnp.zeros((128, 128), jnp.bfloat16)
    limit = weights.shape[0] - 1
    most = panel.shape[0] - 64

    def issue(chunk, unit, totals):
        first_right, second_right = (
            weights[jnp.clip(rights[chunk + side] - first_group, 0, limit)] for side in range(2)
        )
        pltpu.matmul_push_rhs(
            jnp.concatenate(
                [
                    jnp.concatenate([first_right, zero], 1),
                    jnp.concatenate([zero, second_right], 1),
                ],
                0,
            ),
            0,
            unit,
        )
        for task, total in enumerate(totals):
            sides = []
            for side in range(2):
                row = jnp.minimum(lefts[(chunk + side) * CHUNK + task], most)
                sides.append(panel[pl.ds(pl.multiple_of(row, 64), 64), :])
            pltpu.matmul_acc_lhs(
                total, jnp.concatenate(sides, 1), load_staged_rhs=0 if task == 0 else None
            )

    def drain(chunk, unit, totals):
        for task, total in enumerate(totals):
            product = pltpu.matmul_pop(total)
            for side in range(2):
                row = outs[(chunk + side) * CHUNK + task]
                rows = pl.ds(pl.multiple_of(row, 64), 64)
                sums[unit][rows, :] += product[:, side * 128 : side * 128 + 128]

    def work(*totals):
        totals = [totals[index : index + CHUNK] for index in range(0, len(totals), CHUNK)]
        begin, turns = first[segs[0]] * TURN, turn_count[segs[0]]
        for seg in segs[1:]:
            turns = turns + turn_count[seg]
        for unit in range(2):
            issue(begin + 2 * unit, unit, totals[unit])

        @pl.loop(0, turns)
        def _(turn):
            chunk = begin + turn * TURN
            for unit in range(2):
                issue(chunk + 4 + 2 * unit, unit, totals[2 + unit])
            for unit in range(2):
                drain(chunk + 2 * unit, unit, totals[unit])
            for unit in range(2):
                issue(chunk + 8 + 2 * unit, unit, totals[unit])
            for unit in range(2):
                drain(chunk + 4 + 2 * unit, unit, totals[2 + unit])

        for unit in range(2):
            for total in totals[unit]:
                pltpu.matmul_pop(total)

    pl.run_scoped(
        work,
        *[
            pltpu.ACC(unit)((64, 256), jnp.float32)
            for _ in range(2)
            for unit in range(2)
            for _ in range(CHUNK)
        ],
    )

    if not last:
        results[0][...] = sum_0[...] + sum_1[...]
        return
    low = low_half(32)
    for block in range(slots):
        rows = pl.ds(block * 64, 64)
        value = sum_0[rows, :] + sum_1[rows, :]
        value = value + pltpu.roll(value, 64, 1)
        folded[pl.ds(block * 32, 32), :] = jnp.where(low, value[:32], value[32:])
    layer = lax.axis_index("depth")
    size = results[0].shape[0]
    layers = slots // size
    for index, result in enumerate(results):
        row = (layer * size if index == 0 else lax.rem(layer + 1, layers) * size) * 32
        for high in range(0, size, 8):
            for pair in range(32):
                result[high : high + 8, pair * 128 : pair * 128 + 128] = folded[
                    pl.ds(row + high * 32 + pair, 8, stride=32), :
                ]


def tile_sum(tasks, seg, seg_count, left_raw, right_raw, panel, given, sum_in, last, slots, width, first_group, keep=False):
    f32, bf16 = jnp.float32, jnp.bfloat16
    plans = [tasks[name] for name in ("first", "turns", "rights", "left", "out")]
    args = [*plans, *left_raw, *right_raw]
    smem, vmem = pl.BlockSpec(memory_space=pltpu.SMEM), pl.BlockSpec(memory_space=pltpu.VMEM)
    extra = [v for v in [panel, *given, sum_in] if v is not None]
    in_specs = [smem] * 5 + [vmem] * (len(left_raw) + len(right_raw) + len(extra))
    sum_shape = ((slots + 1) * 64, 128)
    shapes = (
        [jax.ShapeDtypeStruct((OUT_DEV, width), f32)] * 2
        if last
        else [jax.ShapeDtypeStruct(sum_shape, f32)]
    )
    blocks = len(left_raw) * 1024 + (0 if panel is None else panel.shape[0])
    scratch = []
    if left_raw and keep:
        shapes.append(jax.ShapeDtypeStruct((blocks, 128), bf16))
    elif left_raw:
        scratch = [pltpu.VMEM((blocks, 128), bf16)]
    if right_raw:
        shapes.append(jax.ShapeDtypeStruct((len(right_raw) * 16, 128, 128), bf16))
    body = functools.partial(
        kernel,
        len(left_raw),
        len(right_raw),
        panel is not None,
        len(given),
        sum_in is not None,
        last,
        slots,
        first_group,
        tuple(range(seg, seg + seg_count)),
        keep,
    )
    return pl.pallas_call(
        lambda *refs: body(refs),
        out_shape=shapes,
        in_specs=in_specs,
        out_specs=[vmem] * len(shapes),
        scratch_shapes=[
            *scratch,
            pltpu.VMEM((512, 128), f32),
            pltpu.VMEM((256, 128), f32),
            pltpu.VMEM((slots * 32 if last else 8, 128), f32),
            pltpu.VMEM(sum_shape, f32),
            pltpu.VMEM(sum_shape, f32),
        ],
        compiler_params=pltpu.CompilerParams(vmem_limit_bytes=44 << 20),
    )(*args, *extra)


def local(
    density,
    square_left,
    square_right,
    square_out,
    square_count,
    cube_left,
    cube_right,
    cube_out,
    cube_count,
):
    per_dev, width = density.shape
    rows, cols, layers = (lax.axis_size(name) for name in ("row", "col", "depth"))
    row, col, layer = (lax.axis_index(name) for name in ("row", "col", "depth"))
    slots = layers * OUT_DEV
    tasks = square_left.shape[0]
    place = jnp.arange(tasks, dtype=jnp.int32)

    def moved_left(left):
        from_col = lax.rem(col - left // (layers * per_dev) + cols, cols)
        from_layer = lax.rem(layer - left // per_dev % layers + layers, layers)
        return from_col, (from_col * layers + from_layer) * per_dev + left % per_dev

    def moved_right(right):
        away = lax.rem(row - right // per_dev + rows, rows)
        order = jnp.where(
            2 * away <= rows - 1 + rows % 2, 2 * away - 1, jnp.minimum(2 * (rows - away), rows - 1)
        )
        return jnp.maximum(order, 0) * per_dev + right % per_dev

    column = [density]
    for _ in range((rows - 1) // 2):
        ahead, behind = (column[-2], column[-1]) if len(column) > 1 else (density, density)
        column += [ring(ahead, "row"), ring(behind, "row", -1)]
    across = ring_all(density, "col")
    lefts = [piece for value in across for piece in ring_all(value, "depth")]

    groups = rows * per_dev
    _, left = moved_left(square_left)
    key = jnp.where(place < square_count[0], moved_right(square_right), groups)
    chunks = -(-(tasks // CHUNK + groups + TURN * rows + TURN) // 16) * 16
    square_tasks = plan(key, left, square_out, groups, per_dev, slots, chunks)
    panel, first = prepare(lefts[:layers], column[:1])
    total, panel = tile_sum(
        square_tasks, 0, 1, lefts[layers:], [], panel, [first], None, False, slots, width, 0, True
    )
    weights = [first]
    if rows % 2 == 0:
        column[-2], total = lax.optimization_barrier((column[-2], total))
        opposite = ring(column[-2] if rows > 2 else density, "row")
    for seg in range(1, len(column), 2):
        last = rows % 2 == 1 and seg + 2 == rows
        *result, piece = tile_sum(
            square_tasks, seg, 2, [], column[seg : seg + 2], panel, [], total, last,
            slots, width, seg * per_dev,
        )
        total = result[0]
        weights.append(piece)

    if rows % 2 == 0:
        *result, piece = tile_sum(
            square_tasks, rows - 1, 1, [], [opposite], panel, [], total, True,
            slots, width, (rows - 1) * per_dev,
        )
        weights.append(piece)
    mine, other = result

    weights = jnp.concatenate(weights, axis=0)
    square = mine + ring(other, "depth")

    cube_left, cube_right, cube_out, cube_count, square = lax.optimization_barrier(
        (cube_left, cube_right, cube_out, cube_count, square)
    )
    from_col, left = moved_left(cube_left)
    left = left - jnp.where(from_col == 0, 0, layers * per_dev)
    key = jnp.where(from_col == 0, 0, groups) + moved_right(cube_right)
    key = jnp.where(place < cube_count[0], key, 2 * groups)
    chunks = -(-(tasks // CHUNK + 2 * groups + TURN * 2 + TURN) // 16) * 16
    cube_tasks = plan(key, left, cube_out, 2 * groups, groups, slots, chunks)

    near = ring_all(square, "depth")
    far = ring_all(square, "col")[1:]
    (total,) = tile_sum(
        cube_tasks, 0, 1, near, [], None, [weights], None, False, slots, width, 0
    )
    total, *far = lax.optimization_barrier((total, *far))
    far = [piece for value in far for piece in ring_all(value, "depth")]
    mine, other = tile_sum(
        cube_tasks, 1, 1, far, [], None, [weights], total, True, slots, width, groups
    )
    cube = mine + ring(other, "depth")
    return 3.0 * square - 2.0 * cube


def solution(mesh):
    return jax.shard_map(
        local,
        mesh=mesh,
        in_specs=(
            P(("groups", "row", "col", "depth"), None),
            P(("groups", "row", "col", "depth")),
            P(("groups", "row", "col", "depth")),
            P(("groups", "row", "col", "depth")),
            P(("groups", "row", "col", "depth")),
            P(("groups", "row", "col", "depth")),
            P(("groups", "row", "col", "depth")),
            P(("groups", "row", "col", "depth")),
            P(("groups", "row", "col", "depth")),
        ),
        out_specs=P(("groups", "row", "col", "depth"), None),
        check_vma=False,
    )
```

```python
import functools
import math

import jax
import jax.numpy as jnp
from jax import lax
from jax.experimental import pallas as pl
from jax.experimental.pallas import tpu as pltpu
from jax.sharding import PartitionSpec as P

OUT_DEV = 16
CHUNK = 8
TURN = 8


def ring(value, axis, step=1):
    size = lax.axis_size(axis)
    return lax.ppermute(value, axis, [(i, (i + step) % size) for i in range(size)])


def ring_all(value, axis):
    pieces = [value]
    for _ in range(lax.axis_size(axis) - 1):
        pieces.append(ring(pieces[-1], axis))
    return pieces


def plan(key, left, out, groups, seg_groups, slots, chunks):
    tasks = key.shape[0]
    place = jnp.arange(tasks, dtype=jnp.int32)
    group = jnp.arange(groups, dtype=jnp.int32)
    segs = groups // seg_groups
    same = (key[:, None] == key[None, :]) & (place[:, None] < place[None, :])
    rank = jnp.sum(same.astype(jnp.int32), axis=0)
    count = jnp.sum((key[:, None] == group[None, :]).astype(jnp.int32), axis=0)
    filled = (count + CHUNK - 1) // CHUNK
    seg_id = group // seg_groups
    earlier = (group[:, None] < group[None, :]) & (seg_id[:, None] == seg_id[None, :])
    within = jnp.sum(jnp.where(earlier, filled[:, None], 0), axis=0)
    total = jnp.sum(filled.reshape(segs, seg_groups), axis=1)
    turns = (total + TURN - 1) // TURN
    seg = jnp.arange(segs, dtype=jnp.int32)
    first = jnp.sum(jnp.where(seg[:, None] < seg[None, :], turns[:, None], 0), axis=0)
    base = within + TURN * jnp.sum(
        jnp.where(seg_id[:, None] == seg[None, :], first[None, :], 0), axis=1
    )
    start = jnp.sum(jnp.where(key[:, None] == group[None, :], base[None, :] * CHUNK, 0), axis=1)
    position = jnp.where(key < groups, start + rank, -1)
    slot = jnp.arange(chunks * CHUNK, dtype=jnp.int32)
    code = jnp.sum(
        jnp.where(
            position[:, None] == slot[None, :], (left * (slots + 1) + out - slots)[:, None], 0
        ),
        axis=0,
    ) + slots
    chunk = jnp.arange(chunks, dtype=jnp.int32)
    rights = jnp.sum((base + filled)[:, None] <= chunk[None, :], axis=0, dtype=jnp.int32)
    return dict(
        first=first,
        turns=turns,
        rights=rights,
        left=code // (slots + 1) * 64,
        out=code % (slots + 1) * 64,
    )


def spread(source, flat):
    for high in range(0, source.shape[0], 8):
        for pair in range(32):
            flat[pl.ds(high * 32 + pair, 8, stride=32), :] = source[
                high : high + 8, pair * 128 : pair * 128 + 128
            ]


def low_half(rows):
    return lax.broadcasted_iota(jnp.int32, (rows, 128), 1) < 64


def split(value):
    top = value.astype(jnp.bfloat16).astype(jnp.float32)
    return top, value - top


def fill_panel(sources, panel, first, flat):
    low = low_half(32)
    for index, source in enumerate(sources):
        spread(source, flat)
        for block in range(16):
            row = (first + index) * 1024 + block * 64
            top, rest = split(flat[block * 32 : block * 32 + 32, :])
            even = jnp.where(low, top, pltpu.roll(rest, 64, 1))
            odd = jnp.where(low, pltpu.roll(top, 64, 1), rest)
            panel[pl.ds(row, 32), :] = even.astype(jnp.bfloat16)
            panel[pl.ds(row + 32, 32), :] = odd.astype(jnp.bfloat16)


def fill_weights(sources, weights, first, flat, tall):
    low, low_tall = low_half(32), low_half(64)
    for index, source in enumerate(sources):
        spread(source, flat)
        for block in range(16):
            both = flat[block * 32 : block * 32 + 32, :]
            swapped = pltpu.roll(both, 64, 1)
            spot = block % 4 * 64
            tall[pl.ds(spot, 32, stride=2), :] = jnp.where(low, both, swapped)
            tall[pl.ds(spot + 1, 32, stride=2), :] = jnp.where(low, swapped, both)
            top, rest = split(tall[spot : spot + 64, :])
            weights[first + index * 16 + block, 0:64] = jnp.where(low_tall, top, rest).astype(jnp.bfloat16)
            weights[first + index * 16 + block, 64:128] = jnp.where(low_tall, top, 0.0).astype(jnp.bfloat16)


def prepare_kernel(raw_lefts, *refs):
    sources, (panel, weights, flat, tall) = refs[:-4], refs[-4:]
    fill_panel(sources[:raw_lefts], panel, 0, flat)
    fill_weights(sources[raw_lefts:], weights, 0, flat, tall)


def extend_kernel(known, *refs):
    sources, (panel, flat) = refs[:-2], refs[-2:]
    size = known.shape[0]
    panel[:size, :] = known[...]
    fill_panel(sources, panel, size // 1024, flat)


def prepare(lefts, rights):
    vmem = pl.BlockSpec(memory_space=pltpu.VMEM)
    return pl.pallas_call(
        functools.partial(prepare_kernel, len(lefts)),
        out_shape=[
            jax.ShapeDtypeStruct((len(lefts) * 1024, 128), jnp.bfloat16),
            jax.ShapeDtypeStruct((len(rights) * 16, 128, 128), jnp.bfloat16),
        ],
        in_specs=[vmem] * (len(lefts) + len(rights)),
        out_specs=[vmem] * 2,
        scratch_shapes=[pltpu.VMEM((size, 128), jnp.float32) for size in (512, 256)],
        compiler_params=pltpu.CompilerParams(vmem_limit_bytes=44 << 20),
    )(*lefts, *rights)


def extend(panel, lefts):
    vmem = pl.BlockSpec(memory_space=pltpu.VMEM)
    rows = panel.shape[0] + len(lefts) * 1024
    return pl.pallas_call(
        extend_kernel,
        out_shape=jax.ShapeDtypeStruct((rows, 128), jnp.bfloat16),
        in_specs=[vmem] * (1 + len(lefts)),
        out_specs=vmem,
        scratch_shapes=[pltpu.VMEM((512, 128), jnp.float32)],
        compiler_params=pltpu.CompilerParams(vmem_limit_bytes=44 << 20),
    )(panel, *lefts)


def kernel(raw_lefts, raw_rights, has_left, has_right, has_sum, last, slots, first_group, segs, keep, refs):
    refs = list(refs)
    first, turn_count, rights, lefts, outs = refs[:5]
    refs = refs[5:]
    left_raw, refs = refs[:raw_lefts], refs[raw_lefts:]
    right_raw, refs = refs[:raw_rights], refs[raw_rights:]
    panel, given, sum_in = None, [], None
    if has_left:
        panel, refs = refs[0], refs[1:]
    given, refs = refs[:has_right], refs[has_right:]
    if has_sum:
        sum_in, refs = refs[0], refs[1:]
    results, refs = refs[:2] if last else refs[:1], refs[2:] if last else refs[1:]
    flat, tall, folded, sum_0, sum_1 = refs[-5:]
    start = 0
    if raw_lefts:
        whole, refs = refs[0], refs[1:]
        if has_left:
            start = panel.shape[0] // 1024
            whole[: panel.shape[0], :] = panel[...]
        panel = whole
    weights = refs[0] if raw_rights else given[0]
    sums = (sum_0, sum_1)
    fill_panel(left_raw, panel, start, flat)
    known = 0
    if raw_rights and has_right:
        known = given[0].shape[0]
        weights[:known] = given[0][...]
    fill_weights(right_raw, weights, known, flat, tall)

    sum_1[...] = jnp.zeros_like(sum_1)
    if has_sum:
        sum_0[...] = sum_in[...]
    else:
        sum_0[...] = jnp.zeros_like(sum_0)

    zero = jnp.zeros((128, 128), jnp.bfloat16)
    limit = weights.shape[0] - 1
    most = panel.shape[0] - 64

    def issue(chunk, unit, totals):
        first_right, second_right = (
            weights[jnp.clip(rights[chunk + side] - first_group, 0, limit)] for side in range(2)
        )
        pltpu.matmul_push_rhs(
            jnp.concatenate(
                [
                    jnp.concatenate([first_right, zero], 1),
                    jnp.concatenate([zero, second_right], 1),
                ],
                0,
            ),
            0,
            unit,
        )
        for task, total in enumerate(totals):
            sides = []
            for side in range(2):
                row = jnp.minimum(lefts[(chunk + side) * CHUNK + task], most)
                sides.append(panel[pl.ds(pl.multiple_of(row, 64), 64), :])
            pltpu.matmul_acc_lhs(
                total, jnp.concatenate(sides, 1), load_staged_rhs=0 if task == 0 else None
            )

    def drain(chunk, unit, totals):
        for task, total in enumerate(totals):
            product = pltpu.matmul_pop(total)
            for side in range(2):
                row = outs[(chunk + side) * CHUNK + task]
                rows = pl.ds(pl.multiple_of(row, 64), 64)
                sums[unit][rows, :] += product[:, side * 128 : side * 128 + 128]

    def work(*totals):
        totals = [totals[index : index + CHUNK] for index in range(0, len(totals), CHUNK)]
        begin, turns = first[segs[0]] * TURN, turn_count[segs[0]]
        for seg in segs[1:]:
            turns = turns + turn_count[seg]
        for unit in range(2):
            issue(begin + 2 * unit, unit, totals[unit])

        @pl.loop(0, turns)
        def _(turn):
            chunk = begin + turn * TURN
            for unit in range(2):
                issue(chunk + 4 + 2 * unit, unit, totals[2 + unit])
            for unit in range(2):
                drain(chunk + 2 * unit, unit, totals[unit])
            for unit in range(2):
                issue(chunk + 8 + 2 * unit, unit, totals[unit])
            for unit in range(2):
                drain(chunk + 4 + 2 * unit, unit, totals[2 + unit])

        for unit in range(2):
            for total in totals[unit]:
                pltpu.matmul_pop(total)

    pl.run_scoped(
        work,
        *[
            pltpu.ACC(unit)((64, 256), jnp.float32)
            for _ in range(2)
            for unit in range(2)
            for _ in range(CHUNK)
        ],
    )

    if not last:
        results[0][...] = sum_0[...] + sum_1[...]
        return
    low = low_half(32)
    for block in range(slots):
        rows = pl.ds(block * 64, 64)
        value = sum_0[rows, :] + sum_1[rows, :]
        value = value + pltpu.roll(value, 64, 1)
        folded[pl.ds(block * 32, 32), :] = jnp.where(low, value[:32], value[32:])
    layer = lax.axis_index("depth")
    size = results[0].shape[0]
    layers = slots // size
    for index, result in enumerate(results):
        row = (layer * size if index == 0 else lax.rem(layer + 1, layers) * size) * 32
        for high in range(0, size, 8):
            for pair in range(32):
                result[high : high + 8, pair * 128 : pair * 128 + 128] = folded[
                    pl.ds(row + high * 32 + pair, 8, stride=32), :
                ]


def tile_sum(tasks, seg, seg_count, left_raw, right_raw, panel, given, sum_in, last, slots, width, first_group, keep=False):
    f32, bf16 = jnp.float32, jnp.bfloat16
    plans = [tasks[name] for name in ("first", "turns", "rights", "left", "out")]
    args = [*plans, *left_raw, *right_raw]
    smem, vmem = pl.BlockSpec(memory_space=pltpu.SMEM), pl.BlockSpec(memory_space=pltpu.VMEM)
    extra = [v for v in [panel, *given, sum_in] if v is not None]
    in_specs = [smem] * 5 + [vmem] * (len(left_raw) + len(right_raw) + len(extra))
    sum_shape = ((slots + 1) * 64, 128)
    shapes = (
        [jax.ShapeDtypeStruct((OUT_DEV, width), f32)] * 2
        if last
        else [jax.ShapeDtypeStruct(sum_shape, f32)]
    )
    blocks = len(left_raw) * 1024 + (0 if panel is None else panel.shape[0])
    scratch = []
    if left_raw and keep:
        shapes.append(jax.ShapeDtypeStruct((blocks, 128), bf16))
    elif left_raw:
        scratch = [pltpu.VMEM((blocks, 128), bf16)]
    if right_raw:
        blocks = len(right_raw) * 16 + sum(value.shape[0] for value in given)
        shapes.append(jax.ShapeDtypeStruct((blocks, 128, 128), bf16))
    body = functools.partial(
        kernel,
        len(left_raw),
        len(right_raw),
        panel is not None,
        len(given),
        sum_in is not None,
        last,
        slots,
        first_group,
        tuple(range(seg, seg + seg_count)),
        keep,
    )
    return pl.pallas_call(
        lambda *refs: body(refs),
        out_shape=shapes,
        in_specs=in_specs,
        out_specs=[vmem] * len(shapes),
        scratch_shapes=[
            *scratch,
            pltpu.VMEM((512, 128), f32),
            pltpu.VMEM((256, 128), f32),
            pltpu.VMEM((slots * 32 if last else 8, 128), f32),
            pltpu.VMEM(sum_shape, f32),
            pltpu.VMEM(sum_shape, f32),
        ],
        compiler_params=pltpu.CompilerParams(vmem_limit_bytes=44 << 20),
    )(*args, *extra)


def local(
    density,
    square_left,
    square_right,
    square_out,
    square_count,
    cube_left,
    cube_right,
    cube_out,
    cube_count,
):
    per_dev, width = density.shape
    rows, cols, layers = (lax.axis_size(name) for name in ("row", "col", "depth"))
    row, col, layer = (lax.axis_index(name) for name in ("row", "col", "depth"))
    slots = layers * OUT_DEV
    tasks = square_left.shape[0]
    place = jnp.arange(tasks, dtype=jnp.int32)

    def moved_left(left):
        from_col = lax.rem(col - left // (layers * per_dev) + cols, cols)
        from_layer = lax.rem(layer - left // per_dev % layers + layers, layers)
        return from_col, (from_col * layers + from_layer) * per_dev + left % per_dev

    def moved_right(right):
        away = lax.rem(row - right // per_dev + rows, rows)
        order = jnp.where(
            2 * away <= rows - 1 + rows % 2, 2 * away - 1, jnp.minimum(2 * (rows - away), rows - 1)
        )
        return jnp.maximum(order, 0) * per_dev + right % per_dev

    column = [density]
    for _ in range((rows - 1) // 2):
        ahead, behind = (column[-2], column[-1]) if len(column) > 1 else (density, density)
        column += [ring(ahead, "row"), ring(behind, "row", -1)]
    across = ring_all(density, "col")
    lefts = [piece for value in across for piece in ring_all(value, "depth")]

    groups = rows * per_dev
    _, left = moved_left(square_left)
    key = jnp.where(place < square_count[0], moved_right(square_right), groups)
    chunks = -(-(tasks // CHUNK + groups + TURN * rows + TURN) // 16) * 16
    square_tasks = plan(key, left, square_out, groups, per_dev, slots, chunks)
    panel, first = prepare(lefts[:layers], column[:1])
    panel = extend(panel, lefts[layers:])
    if rows % 2 == 0:
        column[-2], panel = lax.optimization_barrier((column[-2], panel))
        opposite = ring(column[-2] if rows > 2 else density, "row")
    total, known, weights = None, [first], []
    for seg in range(1, len(column), 2):
        last = rows % 2 == 1 and seg + 2 == rows
        begin = seg - len(known)
        *result, piece = tile_sum(
            square_tasks, begin, seg + 2 - begin, [], column[seg : seg + 2], panel, known, total,
            last, slots, width, begin * per_dev,
        )
        total, known = result[0], []
        weights.append(piece)
    if rows % 2 == 0:
        *result, piece = tile_sum(
            square_tasks, rows - 1, 1, [], [opposite], panel, [], total, True,
            slots, width, (rows - 1) * per_dev,
        )
        weights.append(piece)
    mine, other = result

    weights = jnp.concatenate(weights, axis=0)
    square = mine + ring(other, "depth")

    cube_left, cube_right, cube_out, cube_count, square = lax.optimization_barrier(
        (cube_left, cube_right, cube_out, cube_count, square)
    )
    from_col, left = moved_left(cube_left)
    left = left - jnp.where(from_col == 0, 0, layers * per_dev)
    key = jnp.where(from_col == 0, 0, groups) + moved_right(cube_right)
    key = jnp.where(place < cube_count[0], key, 2 * groups)
    chunks = -(-(tasks // CHUNK + 2 * groups + TURN * 2 + TURN) // 16) * 16
    cube_tasks = plan(key, left, cube_out, 2 * groups, groups, slots, chunks)

    near = ring_all(square, "depth")
    far = ring_all(square, "col")[1:]
    (total,) = tile_sum(
        cube_tasks, 0, 1, near, [], None, [weights], None, False, slots, width, 0
    )
    total, *far = lax.optimization_barrier((total, *far))
    far = [piece for value in far for piece in ring_all(value, "depth")]
    mine, other = tile_sum(
        cube_tasks, 1, 1, far, [], None, [weights], total, True, slots, width, groups
    )
    cube = mine + ring(other, "depth")
    return 3.0 * square - 2.0 * cube


def solution(mesh):
    return jax.shard_map(
        local,
        mesh=mesh,
        in_specs=(
            P(("groups", "row", "col", "depth"), None),
            P(("groups", "row", "col", "depth")),
            P(("groups", "row", "col", "depth")),
            P(("groups", "row", "col", "depth")),
            P(("groups", "row", "col", "depth")),
            P(("groups", "row", "col", "depth")),
            P(("groups", "row", "col", "depth")),
            P(("groups", "row", "col", "depth")),
            P(("groups", "row", "col", "depth")),
        ),
        out_specs=P(("groups", "row", "col", "depth"), None),
        check_vma=False,
    )
```

```python
import functools
import math

import jax
import jax.numpy as jnp
from jax import lax
from jax.experimental import pallas as pl
from jax.experimental.pallas import tpu as pltpu
from jax.sharding import PartitionSpec as P

OUT_DEV = 16
CHUNK = 8
TURN = 8


def ring(value, axis, step=1):
    size = lax.axis_size(axis)
    return lax.ppermute(value, axis, [(i, (i + step) % size) for i in range(size)])


def ring_all(value, axis):
    pieces = [value]
    for _ in range(lax.axis_size(axis) - 1):
        pieces.append(ring(pieces[-1], axis))
    return pieces


def plan(key, left, out, groups, seg_groups, slots, chunks):
    tasks = key.shape[0]
    place = jnp.arange(tasks, dtype=jnp.int32)
    group = jnp.arange(groups, dtype=jnp.int32)
    segs = groups // seg_groups
    same = (key[:, None] == key[None, :]) & (place[:, None] < place[None, :])
    rank = jnp.sum(same.astype(jnp.int32), axis=0)
    count = jnp.sum((key[:, None] == group[None, :]).astype(jnp.int32), axis=0)
    filled = (count + CHUNK - 1) // CHUNK
    seg_id = group // seg_groups
    earlier = (group[:, None] < group[None, :]) & (seg_id[:, None] == seg_id[None, :])
    within = jnp.sum(jnp.where(earlier, filled[:, None], 0), axis=0)
    total = jnp.sum(filled.reshape(segs, seg_groups), axis=1)
    turns = (total + TURN - 1) // TURN
    seg = jnp.arange(segs, dtype=jnp.int32)
    first = jnp.sum(jnp.where(seg[:, None] < seg[None, :], turns[:, None], 0), axis=0)
    base = within + TURN * jnp.sum(
        jnp.where(seg_id[:, None] == seg[None, :], first[None, :], 0), axis=1
    )
    start = jnp.sum(jnp.where(key[:, None] == group[None, :], base[None, :] * CHUNK, 0), axis=1)
    position = jnp.where(key < groups, start + rank, -1)
    slot = jnp.arange(chunks * CHUNK, dtype=jnp.int32)
    code = jnp.sum(
        jnp.where(
            position[:, None] == slot[None, :], (left * (slots + 1) + out - slots)[:, None], 0
        ),
        axis=0,
    ) + slots
    chunk = jnp.arange(chunks, dtype=jnp.int32)
    rights = jnp.sum((base + filled)[:, None] <= chunk[None, :], axis=0, dtype=jnp.int32)
    return dict(
        first=first,
        turns=turns,
        rights=rights,
        left=code // (slots + 1) * 64,
        out=code % (slots + 1) * 64,
    )


def spread(source, flat):
    for high in range(0, source.shape[0], 8):
        for pair in range(32):
            flat[pl.ds(high * 32 + pair, 8, stride=32), :] = source[
                high : high + 8, pair * 128 : pair * 128 + 128
            ]


def low_half(rows):
    return lax.broadcasted_iota(jnp.int32, (rows, 128), 1) < 64


def split(value):
    top = value.astype(jnp.bfloat16).astype(jnp.float32)
    return top, value - top


def fill_panel(sources, panel, first, flat):
    low = low_half(32)
    for index, source in enumerate(sources):
        spread(source, flat)
        for block in range(16):
            row = (first + index) * 1024 + block * 64
            top, rest = split(flat[block * 32 : block * 32 + 32, :])
            even = jnp.where(low, top, pltpu.roll(rest, 64, 1))
            odd = jnp.where(low, pltpu.roll(top, 64, 1), rest)
            panel[pl.ds(row, 32), :] = even.astype(jnp.bfloat16)
            panel[pl.ds(row + 32, 32), :] = odd.astype(jnp.bfloat16)


def fill_weights(sources, weights, first, flat, tall):
    low, low_tall = low_half(32), low_half(64)
    for index, source in enumerate(sources):
        spread(source, flat)
        for block in range(16):
            both = flat[block * 32 : block * 32 + 32, :]
            swapped = pltpu.roll(both, 64, 1)
            spot = block % 4 * 64
            tall[pl.ds(spot, 32, stride=2), :] = jnp.where(low, both, swapped)
            tall[pl.ds(spot + 1, 32, stride=2), :] = jnp.where(low, swapped, both)
            top, rest = split(tall[spot : spot + 64, :])
            weights[first + index * 16 + block, 0:64] = jnp.where(low_tall, top, rest).astype(jnp.bfloat16)
            weights[first + index * 16 + block, 64:128] = jnp.where(low_tall, top, 0.0).astype(jnp.bfloat16)


def prepare_kernel(raw_lefts, *refs):
    sources, (panel, weights, flat, tall) = refs[:-4], refs[-4:]
    fill_panel(sources[:raw_lefts], panel, 0, flat)
    fill_weights(sources[raw_lefts:], weights, 0, flat, tall)


def extend_kernel(known, *refs):
    sources, (panel, flat) = refs[:-2], refs[-2:]
    size = known.shape[0]
    panel[:size, :] = known[...]
    fill_panel(sources, panel, size // 1024, flat)


def prepare(lefts, rights):
    vmem = pl.BlockSpec(memory_space=pltpu.VMEM)
    return pl.pallas_call(
        functools.partial(prepare_kernel, len(lefts)),
        out_shape=[
            jax.ShapeDtypeStruct((len(lefts) * 1024, 128), jnp.bfloat16),
            jax.ShapeDtypeStruct((len(rights) * 16, 128, 128), jnp.bfloat16),
        ],
        in_specs=[vmem] * (len(lefts) + len(rights)),
        out_specs=[vmem] * 2,
        scratch_shapes=[pltpu.VMEM((size, 128), jnp.float32) for size in (512, 256)],
        compiler_params=pltpu.CompilerParams(vmem_limit_bytes=44 << 20),
    )(*lefts, *rights)


def extend(panel, lefts):
    vmem = pl.BlockSpec(memory_space=pltpu.VMEM)
    rows = panel.shape[0] + len(lefts) * 1024
    return pl.pallas_call(
        extend_kernel,
        out_shape=jax.ShapeDtypeStruct((rows, 128), jnp.bfloat16),
        in_specs=[vmem] * (1 + len(lefts)),
        out_specs=vmem,
        scratch_shapes=[pltpu.VMEM((512, 128), jnp.float32)],
        compiler_params=pltpu.CompilerParams(vmem_limit_bytes=44 << 20),
    )(panel, *lefts)


def kernel(raw_lefts, raw_rights, has_left, has_right, has_sum, last, slots, first_group, segs, keep, refs):
    refs = list(refs)
    first, turn_count, rights, lefts, outs = refs[:5]
    refs = refs[5:]
    left_raw, refs = refs[:raw_lefts], refs[raw_lefts:]
    right_raw, refs = refs[:raw_rights], refs[raw_rights:]
    panel, given, sum_in = None, [], None
    if has_left:
        panel, refs = refs[0], refs[1:]
    given, refs = refs[:has_right], refs[has_right:]
    if has_sum:
        sum_in, refs = refs[0], refs[1:]
    results, refs = refs[:2] if last else refs[:1], refs[2:] if last else refs[1:]
    flat, tall, folded, sum_0, sum_1 = refs[-5:]
    start = 0
    if raw_lefts:
        whole, refs = refs[0], refs[1:]
        if has_left:
            start = panel.shape[0] // 1024
            whole[: panel.shape[0], :] = panel[...]
        panel = whole
    weights = refs[0] if raw_rights else given[0]
    sums = (sum_0, sum_1)
    fill_panel(left_raw, panel, start, flat)
    known = 0
    if raw_rights and has_right:
        known = given[0].shape[0]
        weights[:known] = given[0][...]
    fill_weights(right_raw, weights, known, flat, tall)

    sum_1[...] = jnp.zeros_like(sum_1)
    if has_sum:
        sum_0[...] = sum_in[...]
    else:
        sum_0[...] = jnp.zeros_like(sum_0)

    zero = jnp.zeros((128, 128), jnp.bfloat16)
    limit = weights.shape[0] - 1
    most = panel.shape[0] - 64

    def issue(chunk, unit, totals):
        first_right, second_right = (
            weights[jnp.clip(rights[chunk + side] - first_group, 0, limit)] for side in range(2)
        )
        pltpu.matmul_push_rhs(
            jnp.concatenate(
                [
                    jnp.concatenate([first_right, zero], 1),
                    jnp.concatenate([zero, second_right], 1),
                ],
                0,
            ),
            0,
            unit,
        )
        for task, total in enumerate(totals):
            sides = []
            for side in range(2):
                row = jnp.minimum(lefts[(chunk + side) * CHUNK + task], most)
                sides.append(panel[pl.ds(pl.multiple_of(row, 64), 64), :])
            pltpu.matmul_acc_lhs(
                total, jnp.concatenate(sides, 1), load_staged_rhs=0 if task == 0 else None
            )

    def drain(chunk, unit, totals):
        for task, total in enumerate(totals):
            product = pltpu.matmul_pop(total)
            for side in range(2):
                row = outs[(chunk + side) * CHUNK + task]
                rows = pl.ds(pl.multiple_of(row, 64), 64)
                sums[unit][rows, :] += product[:, side * 128 : side * 128 + 128]

    def work(*totals):
        totals = [totals[index : index + CHUNK] for index in range(0, len(totals), CHUNK)]
        begin, turns = first[segs[0]] * TURN, turn_count[segs[0]]
        for seg in segs[1:]:
            turns = turns + turn_count[seg]
        for unit in range(2):
            issue(begin + 2 * unit, unit, totals[unit])

        @pl.loop(0, turns)
        def _(turn):
            chunk = begin + turn * TURN
            for unit in range(2):
                issue(chunk + 4 + 2 * unit, unit, totals[2 + unit])
            for unit in range(2):
                drain(chunk + 2 * unit, unit, totals[unit])
            for unit in range(2):
                issue(chunk + 8 + 2 * unit, unit, totals[unit])
            for unit in range(2):
                drain(chunk + 4 + 2 * unit, unit, totals[2 + unit])

        for unit in range(2):
            for total in totals[unit]:
                pltpu.matmul_pop(total)

    pl.run_scoped(
        work,
        *[
            pltpu.ACC(unit)((64, 256), jnp.float32)
            for _ in range(2)
            for unit in range(2)
            for _ in range(CHUNK)
        ],
    )

    if not last:
        results[0][...] = sum_0[...] + sum_1[...]
        return
    low = low_half(32)
    for block in range(slots):
        rows = pl.ds(block * 64, 64)
        value = sum_0[rows, :] + sum_1[rows, :]
        value = value + pltpu.roll(value, 64, 1)
        folded[pl.ds(block * 32, 32), :] = jnp.where(low, value[:32], value[32:])
    layer = lax.axis_index("depth")
    size = results[0].shape[0]
    layers = slots // size
    for index, result in enumerate(results):
        row = (layer * size if index == 0 else lax.rem(layer + 1, layers) * size) * 32
        for high in range(0, size, 8):
            for pair in range(32):
                result[high : high + 8, pair * 128 : pair * 128 + 128] = folded[
                    pl.ds(row + high * 32 + pair, 8, stride=32), :
                ]


def tile_sum(tasks, seg, seg_count, left_raw, right_raw, panel, given, sum_in, last, slots, width, first_group, keep=False):
    f32, bf16 = jnp.float32, jnp.bfloat16
    plans = [tasks[name] for name in ("first", "turns", "rights", "left", "out")]
    args = [*plans, *left_raw, *right_raw]
    smem, vmem = pl.BlockSpec(memory_space=pltpu.SMEM), pl.BlockSpec(memory_space=pltpu.VMEM)
    extra = [v for v in [panel, *given, sum_in] if v is not None]
    in_specs = [smem] * 5 + [vmem] * (len(left_raw) + len(right_raw) + len(extra))
    sum_shape = ((slots + 1) * 64, 128)
    shapes = (
        [jax.ShapeDtypeStruct((OUT_DEV, width), f32)] * 2
        if last
        else [jax.ShapeDtypeStruct(sum_shape, f32)]
    )
    blocks = len(left_raw) * 1024 + (0 if panel is None else panel.shape[0])
    scratch = []
    if left_raw and keep:
        shapes.append(jax.ShapeDtypeStruct((blocks, 128), bf16))
    elif left_raw:
        scratch = [pltpu.VMEM((blocks, 128), bf16)]
    if right_raw:
        blocks = len(right_raw) * 16 + sum(value.shape[0] for value in given)
        shapes.append(jax.ShapeDtypeStruct((blocks, 128, 128), bf16))
    body = functools.partial(
        kernel,
        len(left_raw),
        len(right_raw),
        panel is not None,
        len(given),
        sum_in is not None,
        last,
        slots,
        first_group,
        tuple(range(seg, seg + seg_count)),
        keep,
    )
    return pl.pallas_call(
        lambda *refs: body(refs),
        out_shape=shapes,
        in_specs=in_specs,
        out_specs=[vmem] * len(shapes),
        scratch_shapes=[
            *scratch,
            pltpu.VMEM((512, 128), f32),
            pltpu.VMEM((256, 128), f32),
            pltpu.VMEM((slots * 32 if last else 8, 128), f32),
            pltpu.VMEM(sum_shape, f32),
            pltpu.VMEM(sum_shape, f32),
        ],
        compiler_params=pltpu.CompilerParams(vmem_limit_bytes=44 << 20),
    )(*args, *extra)


def local(
    density,
    square_left,
    square_right,
    square_out,
    square_count,
    cube_left,
    cube_right,
    cube_out,
    cube_count,
):
    per_dev, width = density.shape
    rows, cols, layers = (lax.axis_size(name) for name in ("row", "col", "depth"))
    row, col, layer = (lax.axis_index(name) for name in ("row", "col", "depth"))
    slots = layers * OUT_DEV
    tasks = square_left.shape[0]
    place = jnp.arange(tasks, dtype=jnp.int32)

    def moved_left(left):
        from_col = lax.rem(col - left // (layers * per_dev) + cols, cols)
        from_layer = lax.rem(layer - left // per_dev % layers + layers, layers)
        return from_col, (from_col * layers + from_layer) * per_dev + left % per_dev

    def moved_right(right):
        away = lax.rem(row - right // per_dev + rows, rows)
        order = jnp.where(
            2 * away <= rows - 1 + rows % 2, 2 * away - 1, jnp.minimum(2 * (rows - away), rows - 1)
        )
        return jnp.maximum(order, 0) * per_dev + right % per_dev

    column = [density]
    for _ in range((rows - 1) // 2):
        ahead, behind = (column[-2], column[-1]) if len(column) > 1 else (density, density)
        column += [ring(ahead, "row"), ring(behind, "row", -1)]
    across = ring_all(density, "col")
    lefts = [piece for value in across for piece in ring_all(value, "depth")]

    groups = rows * per_dev
    _, left = moved_left(square_left)
    key = jnp.where(place < square_count[0], moved_right(square_right), groups)
    chunks = -(-(tasks // CHUNK + groups + TURN * rows + TURN) // 16) * 16
    square_tasks = plan(key, left, square_out, groups, per_dev, slots, chunks)
    panel, first = prepare(lefts[:layers], column[:1])
    panel = extend(panel, lefts[layers:])
    if rows % 2 == 0:
        column[-2], panel = lax.optimization_barrier((column[-2], panel))
        opposite = ring(column[-2] if rows > 2 else density, "row")
    cube_left, cube_right, cube_out, cube_count, panel = lax.optimization_barrier(
        (cube_left, cube_right, cube_out, cube_count, panel)
    )
    from_col, left = moved_left(cube_left)
    left = left - jnp.where(from_col == 0, 0, layers * per_dev)
    key = jnp.where(from_col == 0, 0, groups) + moved_right(cube_right)
    key = jnp.where(place < cube_count[0], key, 2 * groups)
    chunks = -(-(tasks // CHUNK + 2 * groups + TURN * 2 + TURN) // 16) * 16
    cube_tasks = plan(key, left, cube_out, 2 * groups, groups, slots, chunks)

    total, known, weights = None, [first], []
    for seg in range(1, len(column), 2):
        last = rows % 2 == 1 and seg + 2 == rows
        begin = seg - len(known)
        *result, piece = tile_sum(
            square_tasks, begin, seg + 2 - begin, [], column[seg : seg + 2], panel, known, total,
            last, slots, width, begin * per_dev,
        )
        total, known = result[0], []
        weights.append(piece)
    if rows % 2 == 0:
        *result, piece = tile_sum(
            square_tasks, rows - 1, 1, [], [opposite], panel, [], total, True,
            slots, width, (rows - 1) * per_dev,
        )
        weights.append(piece)
    mine, other = result

    weights = jnp.concatenate(weights, axis=0)
    square = mine + ring(other, "depth")

    near = ring_all(square, "depth")
    far = ring_all(square, "col")[1:]
    (total,) = tile_sum(
        cube_tasks, 0, 1, near, [], None, [weights], None, False, slots, width, 0
    )
    total, *far = lax.optimization_barrier((total, *far))
    far = [piece for value in far for piece in ring_all(value, "depth")]
    mine, other = tile_sum(
        cube_tasks, 1, 1, far, [], None, [weights], total, True, slots, width, groups
    )
    cube = mine + ring(other, "depth")
    return 3.0 * square - 2.0 * cube


def solution(mesh):
    return jax.shard_map(
        local,
        mesh=mesh,
        in_specs=(
            P(("groups", "row", "col", "depth"), None),
            P(("groups", "row", "col", "depth")),
            P(("groups", "row", "col", "depth")),
            P(("groups", "row", "col", "depth")),
            P(("groups", "row", "col", "depth")),
            P(("groups", "row", "col", "depth")),
            P(("groups", "row", "col", "depth")),
            P(("groups", "row", "col", "depth")),
            P(("groups", "row", "col", "depth")),
        ),
        out_specs=P(("groups", "row", "col", "depth"), None),
        check_vma=False,
    )
```

```python
import functools
import math

import jax
import jax.numpy as jnp
from jax import lax
from jax.experimental import pallas as pl
from jax.experimental.pallas import tpu as pltpu
from jax.sharding import PartitionSpec as P

OUT_DEV = 16
CHUNK = 8
TURN = 8


def ring(value, axis, step=1):
    size = lax.axis_size(axis)
    return lax.ppermute(value, axis, [(i, (i + step) % size) for i in range(size)])


def ring_all(value, axis):
    pieces = [value]
    for _ in range(lax.axis_size(axis) - 1):
        pieces.append(ring(pieces[-1], axis))
    return pieces


def plan(key, left, out, groups, seg_groups):
    tasks = key.shape[0]
    place = jnp.arange(tasks, dtype=jnp.int32)
    group = jnp.arange(groups, dtype=jnp.int32)
    segs = groups // seg_groups
    same = (key[:, None] == key[None, :]) & (place[:, None] < place[None, :])
    rank = jnp.sum(same.astype(jnp.int32), axis=0)
    count = jnp.sum((key[:, None] == group[None, :]).astype(jnp.int32), axis=0)
    filled = (count + CHUNK - 1) // CHUNK
    seg_id = group // seg_groups
    earlier = (group[:, None] < group[None, :]) & (seg_id[:, None] == seg_id[None, :])
    within = jnp.sum(jnp.where(earlier, filled[:, None], 0), axis=0)
    total = jnp.sum(filled.reshape(segs, seg_groups), axis=1)
    turns = (total + TURN - 1) // TURN
    seg = jnp.arange(segs, dtype=jnp.int32)
    first = jnp.sum(jnp.where(seg[:, None] < seg[None, :], turns[:, None], 0), axis=0)
    base = within + TURN * jnp.sum(
        jnp.where(seg_id[:, None] == seg[None, :], first[None, :], 0), axis=1
    )
    start = jnp.sum(jnp.where(key[:, None] == group[None, :], base[None, :] * CHUNK, 0), axis=1)
    position = jnp.where(key < groups, start + rank, -1)
    return position, left, out, base, filled, first, turns


def slot_lists(placed, slots, chunks):
    position, left, out, base, filled, first, turns = placed
    slot = jnp.arange(chunks * CHUNK, dtype=jnp.int32)
    code = jnp.sum(
        jnp.where(
            position[:, None] == slot[None, :], (left * (slots + 1) + out - slots)[:, None], 0
        ),
        axis=0,
    ) + slots
    chunk = jnp.arange(chunks, dtype=jnp.int32)
    rights = jnp.sum((base + filled)[:, None] <= chunk[None, :], axis=0, dtype=jnp.int32)
    return dict(
        first=first,
        turns=turns,
        rights=rights,
        left=code // (slots + 1) * 64,
        out=code % (slots + 1) * 64,
    )


def spread(source, flat):
    for high in range(0, source.shape[0], 8):
        for pair in range(32):
            flat[pl.ds(high * 32 + pair, 8, stride=32), :] = source[
                high : high + 8, pair * 128 : pair * 128 + 128
            ]


def low_half(rows):
    return lax.broadcasted_iota(jnp.int32, (rows, 128), 1) < 64


def split(value):
    top = value.astype(jnp.bfloat16).astype(jnp.float32)
    return top, value - top


def fill_panel(sources, panel, first, flat):
    low = low_half(32)
    for index, source in enumerate(sources):
        spread(source, flat)
        for block in range(16):
            row = (first + index) * 1024 + block * 64
            top, rest = split(flat[block * 32 : block * 32 + 32, :])
            even = jnp.where(low, top, pltpu.roll(rest, 64, 1))
            odd = jnp.where(low, pltpu.roll(top, 64, 1), rest)
            panel[pl.ds(row, 32), :] = even.astype(jnp.bfloat16)
            panel[pl.ds(row + 32, 32), :] = odd.astype(jnp.bfloat16)


def fill_weights(sources, weights, first, flat, tall):
    low, low_tall = low_half(32), low_half(64)
    for index, source in enumerate(sources):
        spread(source, flat)
        for block in range(16):
            both = flat[block * 32 : block * 32 + 32, :]
            swapped = pltpu.roll(both, 64, 1)
            spot = block % 4 * 64
            tall[pl.ds(spot, 32, stride=2), :] = jnp.where(low, both, swapped)
            tall[pl.ds(spot + 1, 32, stride=2), :] = jnp.where(low, swapped, both)
            top, rest = split(tall[spot : spot + 64, :])
            weights[first + index * 16 + block, 0:64] = jnp.where(low_tall, top, rest).astype(jnp.bfloat16)
            weights[first + index * 16 + block, 64:128] = jnp.where(low_tall, top, 0.0).astype(jnp.bfloat16)


def prepare_kernel(raw_lefts, *refs):
    sources, (panel, weights, flat, tall) = refs[:-4], refs[-4:]
    fill_panel(sources[:raw_lefts], panel, 0, flat)
    fill_weights(sources[raw_lefts:], weights, 0, flat, tall)


def extend_kernel(known, *refs):
    sources, (panel, flat) = refs[:-2], refs[-2:]
    size = known.shape[0]
    panel[:size, :] = known[...]
    fill_panel(sources, panel, size // 1024, flat)


def prepare(lefts, rights):
    vmem = pl.BlockSpec(memory_space=pltpu.VMEM)
    return pl.pallas_call(
        functools.partial(prepare_kernel, len(lefts)),
        out_shape=[
            jax.ShapeDtypeStruct((len(lefts) * 1024, 128), jnp.bfloat16),
            jax.ShapeDtypeStruct((len(rights) * 16, 128, 128), jnp.bfloat16),
        ],
        in_specs=[vmem] * (len(lefts) + len(rights)),
        out_specs=[vmem] * 2,
        scratch_shapes=[pltpu.VMEM((size, 128), jnp.float32) for size in (512, 256)],
        compiler_params=pltpu.CompilerParams(vmem_limit_bytes=44 << 20),
    )(*lefts, *rights)


def extend(panel, lefts):
    vmem = pl.BlockSpec(memory_space=pltpu.VMEM)
    rows = panel.shape[0] + len(lefts) * 1024
    return pl.pallas_call(
        extend_kernel,
        out_shape=jax.ShapeDtypeStruct((rows, 128), jnp.bfloat16),
        in_specs=[vmem] * (1 + len(lefts)),
        out_specs=vmem,
        scratch_shapes=[pltpu.VMEM((512, 128), jnp.float32)],
        compiler_params=pltpu.CompilerParams(vmem_limit_bytes=44 << 20),
    )(panel, *lefts)


def kernel(raw_lefts, raw_rights, has_left, has_right, has_sum, last, slots, first_group, segs, keep, refs):
    refs = list(refs)
    first, turn_count, rights, lefts, outs = refs[:5]
    refs = refs[5:]
    left_raw, refs = refs[:raw_lefts], refs[raw_lefts:]
    right_raw, refs = refs[:raw_rights], refs[raw_rights:]
    panel, given, sum_in = None, [], None
    if has_left:
        panel, refs = refs[0], refs[1:]
    given, refs = refs[:has_right], refs[has_right:]
    if has_sum:
        sum_in, refs = refs[0], refs[1:]
    results, refs = refs[:2] if last else refs[:1], refs[2:] if last else refs[1:]
    flat, tall, folded, sum_0, sum_1 = refs[-5:]
    start = 0
    if raw_lefts:
        whole, refs = refs[0], refs[1:]
        if has_left:
            start = panel.shape[0] // 1024
            whole[: panel.shape[0], :] = panel[...]
        panel = whole
    weights = refs[0] if raw_rights else given[0]
    sums = (sum_0, sum_1)
    fill_panel(left_raw, panel, start, flat)
    known = 0
    if raw_rights and has_right:
        known = given[0].shape[0]
        weights[:known] = given[0][...]
    fill_weights(right_raw, weights, known, flat, tall)

    sum_1[...] = jnp.zeros_like(sum_1)
    if has_sum:
        sum_0[...] = sum_in[...]
    else:
        sum_0[...] = jnp.zeros_like(sum_0)

    zero = jnp.zeros((128, 128), jnp.bfloat16)
    limit = weights.shape[0] - 1
    most = panel.shape[0] - 64

    def issue(chunk, unit, totals):
        first_right, second_right = (
            weights[jnp.clip(rights[chunk + side] - first_group, 0, limit)] for side in range(2)
        )
        pltpu.matmul_push_rhs(
            jnp.concatenate(
                [
                    jnp.concatenate([first_right, zero], 1),
                    jnp.concatenate([zero, second_right], 1),
                ],
                0,
            ),
            0,
            unit,
        )
        for task, total in enumerate(totals):
            sides = []
            for side in range(2):
                row = jnp.minimum(lefts[(chunk + side) * CHUNK + task], most)
                sides.append(panel[pl.ds(pl.multiple_of(row, 64), 64), :])
            pltpu.matmul_acc_lhs(
                total, jnp.concatenate(sides, 1), load_staged_rhs=0 if task == 0 else None
            )

    def drain(chunk, unit, totals):
        for task, total in enumerate(totals):
            product = pltpu.matmul_pop(total)
            for side in range(2):
                row = outs[(chunk + side) * CHUNK + task]
                rows = pl.ds(pl.multiple_of(row, 64), 64)
                sums[unit][rows, :] += product[:, side * 128 : side * 128 + 128]

    def work(*totals):
        totals = [totals[index : index + CHUNK] for index in range(0, len(totals), CHUNK)]
        begin, turns = first[segs[0]] * TURN, turn_count[segs[0]]
        for seg in segs[1:]:
            turns = turns + turn_count[seg]
        for unit in range(2):
            issue(begin + 2 * unit, unit, totals[unit])

        @pl.loop(0, turns)
        def _(turn):
            chunk = begin + turn * TURN
            for unit in range(2):
                issue(chunk + 4 + 2 * unit, unit, totals[2 + unit])
            for unit in range(2):
                drain(chunk + 2 * unit, unit, totals[unit])
            for unit in range(2):
                issue(chunk + 8 + 2 * unit, unit, totals[unit])
            for unit in range(2):
                drain(chunk + 4 + 2 * unit, unit, totals[2 + unit])

        for unit in range(2):
            for total in totals[unit]:
                pltpu.matmul_pop(total)

    pl.run_scoped(
        work,
        *[
            pltpu.ACC(unit)((64, 256), jnp.float32)
            for _ in range(2)
            for unit in range(2)
            for _ in range(CHUNK)
        ],
    )

    if not last:
        results[0][...] = sum_0[...] + sum_1[...]
        return
    low = low_half(32)
    for block in range(slots):
        rows = pl.ds(block * 64, 64)
        value = sum_0[rows, :] + sum_1[rows, :]
        value = value + pltpu.roll(value, 64, 1)
        folded[pl.ds(block * 32, 32), :] = jnp.where(low, value[:32], value[32:])
    layer = lax.axis_index("depth")
    size = results[0].shape[0]
    layers = slots // size
    for index, result in enumerate(results):
        row = (layer * size if index == 0 else lax.rem(layer + 1, layers) * size) * 32
        for high in range(0, size, 8):
            for pair in range(32):
                result[high : high + 8, pair * 128 : pair * 128 + 128] = folded[
                    pl.ds(row + high * 32 + pair, 8, stride=32), :
                ]


def tile_sum(tasks, seg, seg_count, left_raw, right_raw, panel, given, sum_in, last, slots, width, first_group, keep=False):
    f32, bf16 = jnp.float32, jnp.bfloat16
    plans = [tasks[name] for name in ("first", "turns", "rights", "left", "out")]
    args = [*plans, *left_raw, *right_raw]
    smem, vmem = pl.BlockSpec(memory_space=pltpu.SMEM), pl.BlockSpec(memory_space=pltpu.VMEM)
    extra = [v for v in [panel, *given, sum_in] if v is not None]
    in_specs = [smem] * 5 + [vmem] * (len(left_raw) + len(right_raw) + len(extra))
    sum_shape = ((slots + 1) * 64, 128)
    shapes = (
        [jax.ShapeDtypeStruct((OUT_DEV, width), f32)] * 2
        if last
        else [jax.ShapeDtypeStruct(sum_shape, f32)]
    )
    blocks = len(left_raw) * 1024 + (0 if panel is None else panel.shape[0])
    scratch = []
    if left_raw and keep:
        shapes.append(jax.ShapeDtypeStruct((blocks, 128), bf16))
    elif left_raw:
        scratch = [pltpu.VMEM((blocks, 128), bf16)]
    if right_raw:
        blocks = len(right_raw) * 16 + sum(value.shape[0] for value in given)
        shapes.append(jax.ShapeDtypeStruct((blocks, 128, 128), bf16))
    body = functools.partial(
        kernel,
        len(left_raw),
        len(right_raw),
        panel is not None,
        len(given),
        sum_in is not None,
        last,
        slots,
        first_group,
        tuple(range(seg, seg + seg_count)),
        keep,
    )
    return pl.pallas_call(
        lambda *refs: body(refs),
        out_shape=shapes,
        in_specs=in_specs,
        out_specs=[vmem] * len(shapes),
        scratch_shapes=[
            *scratch,
            pltpu.VMEM((512, 128), f32),
            pltpu.VMEM((256, 128), f32),
            pltpu.VMEM((slots * 32 if last else 8, 128), f32),
            pltpu.VMEM(sum_shape, f32),
            pltpu.VMEM(sum_shape, f32),
        ],
        compiler_params=pltpu.CompilerParams(vmem_limit_bytes=44 << 20),
    )(*args, *extra)


def local(
    density,
    square_left,
    square_right,
    square_out,
    square_count,
    cube_left,
    cube_right,
    cube_out,
    cube_count,
):
    per_dev, width = density.shape
    rows, cols, layers = (lax.axis_size(name) for name in ("row", "col", "depth"))
    row, col, layer = (lax.axis_index(name) for name in ("row", "col", "depth"))
    slots = layers * OUT_DEV
    tasks = square_left.shape[0]
    place = jnp.arange(tasks, dtype=jnp.int32)

    def moved_left(left):
        from_col = lax.rem(col - left // (layers * per_dev) + cols, cols)
        from_layer = lax.rem(layer - left // per_dev % layers + layers, layers)
        return from_col, (from_col * layers + from_layer) * per_dev + left % per_dev

    def moved_right(right):
        away = lax.rem(row - right // per_dev + rows, rows)
        order = jnp.where(
            2 * away <= rows - 1 + rows % 2, 2 * away - 1, jnp.minimum(2 * (rows - away), rows - 1)
        )
        return jnp.maximum(order, 0) * per_dev + right % per_dev

    column = [density]
    for _ in range((rows - 1) // 2):
        ahead, behind = (column[-2], column[-1]) if len(column) > 1 else (density, density)
        column += [ring(ahead, "row"), ring(behind, "row", -1)]
    across = ring_all(density, "col")
    lefts = [piece for value in across for piece in ring_all(value, "depth")]

    groups = rows * per_dev
    _, left = moved_left(square_left)
    key = jnp.where(place < square_count[0], moved_right(square_right), groups)
    chunks = -(-(tasks // CHUNK + groups + TURN * rows + TURN) // 16) * 16
    square_tasks = slot_lists(plan(key, left, square_out, groups, per_dev), slots, chunks)
    panel, first = prepare(lefts[:layers], column[:1])
    panel = extend(panel, lefts[layers:])
    if rows % 2 == 0:
        column[-2], panel = lax.optimization_barrier((column[-2], panel))
        opposite = ring(column[-2] if rows > 2 else density, "row")
    cube_left, cube_right, cube_out, cube_count, panel = lax.optimization_barrier(
        (cube_left, cube_right, cube_out, cube_count, panel)
    )
    from_col, left = moved_left(cube_left)
    left = left - jnp.where(from_col == 0, 0, layers * per_dev)
    key = jnp.where(from_col == 0, 0, groups) + moved_right(cube_right)
    key = jnp.where(place < cube_count[0], key, 2 * groups)
    chunks = -(-(tasks // CHUNK + 2 * groups + TURN * 2 + TURN) // 16) * 16
    placed = plan(key, left, cube_out, 2 * groups, groups)

    total, known, weights = None, [first], []
    for seg in range(1, len(column), 2):
        last = rows % 2 == 1 and seg + 2 == rows
        begin = seg - len(known)
        *result, piece = tile_sum(
            square_tasks, begin, seg + 2 - begin, [], column[seg : seg + 2], panel, known, total,
            last, slots, width, begin * per_dev,
        )
        total, known = result[0], []
        weights.append(piece)
    if rows % 2 == 0:
        *result, piece = tile_sum(
            square_tasks, rows - 1, 1, [], [opposite], panel, [], total, True,
            slots, width, (rows - 1) * per_dev,
        )
        weights.append(piece)
    mine, other = result
    position, mine = lax.optimization_barrier((placed[0], mine))
    cube_tasks = slot_lists((position, *placed[1:]), slots, chunks)

    weights = jnp.concatenate(weights, axis=0)
    square = mine + ring(other, "depth")

    near = ring_all(square, "depth")
    far = ring_all(square, "col")[1:]
    (total,) = tile_sum(
        cube_tasks, 0, 1, near, [], None, [weights], None, False, slots, width, 0
    )
    total, *far = lax.optimization_barrier((total, *far))
    far = [piece for value in far for piece in ring_all(value, "depth")]
    mine, other = tile_sum(
        cube_tasks, 1, 1, far, [], None, [weights], total, True, slots, width, groups
    )
    cube = mine + ring(other, "depth")
    return 3.0 * square - 2.0 * cube


def solution(mesh):
    return jax.shard_map(
        local,
        mesh=mesh,
        in_specs=(
            P(("groups", "row", "col", "depth"), None),
            P(("groups", "row", "col", "depth")),
            P(("groups", "row", "col", "depth")),
            P(("groups", "row", "col", "depth")),
            P(("groups", "row", "col", "depth")),
            P(("groups", "row", "col", "depth")),
            P(("groups", "row", "col", "depth")),
            P(("groups", "row", "col", "depth")),
            P(("groups", "row", "col", "depth")),
        ),
        out_specs=P(("groups", "row", "col", "depth"), None),
        check_vma=False,
    )
```
